512 devices in a mesh: shard: 128 (over y, z, core), rep: 4 (over x).
Axes of the slice: x: 4, y: 8, z: 8, core: 2. Of those that a mesh axis runs over, the one named last changes fastest.
Arguments:
- embeds: bfloat16 [65536, 1024], P(('shard', 'rep')), may hold values from -25 to 25
- clusters: int32 [65536], P(('shard', 'rep')), may hold values from 0 to 511, as said below
- orders: int32 [65536], P(('shard', 'rep')), may hold values from 0 to 65535, each once
- owner_map: int32 [512], replicated, may hold values from 0 to 127, as said below
- neighbours: int32 [512, 2], replicated, may hold values from 0 to 511, as said below
Outputs:
- max_similarity: float32 [65536], P(('shard', 'rep'))
The draws below stay inside these ranges and needn't reach their ends.
Inputs may be any that keep to these rules, and one draw needn't show every extreme that they name: The rows of one loader device (aligned blocks of 128 rows) put exactly 2 rows into the clusters of each of 64 owners (owner by owner_map) and none into the others; one owner receives 2 rows from every loader device. `owner_map`: every owner index owns exactly 4 clusters. `neighbours`: row c lists 2 different clusters other than c, each owned by the owner of c or by the owner one index below or above it, counted around the 128 owners.
All inputs are finite; a program needn't handle non-finite values.
Results may differ from the reference program's by a relative error of at most 0.00051.
Values may be sent and summed in bfloat16 or wider, within the bound.
No kernel may reach another device: no remote copies, remote signals or barrier semaphores. Data moves between devices by JAX's collectives and lax.ppermute only.
A program may use at most 64 MiB of HBM per device.

```python
import jax
import jax.numpy as jnp
from jax import lax

D = 1024
ROWS_DEV = 128
CPO = 4
NB = 2
SLOT = 2
CLUSTERS = 512
ROWS = 65536
N_SHARD = 128
N_REP = 4


def placement(key):
    shuffled = jax.random.permutation(jax.random.fold_in(key, 101), CLUSTERS).astype(jnp.int32)
    position = jnp.arange(CLUSTERS, dtype=jnp.int32)
    owner_table = jnp.zeros((CLUSTERS,), jnp.int32).at[shuffled].set(position // CPO)
    return (shuffled, owner_table)


def neighbour_lists(key):
    shuffled, owner_table = placement(key)
    position = jnp.arange(CLUSTERS, dtype=jnp.int32)
    rank_order = jax.random.randint(jax.random.fold_in(key, 102), (CLUSTERS, 3 * CPO - 1), 0, 2 ** 30)
    chosen = jnp.argsort(rank_order, axis=1, stable=True)[:, :NB].astype(jnp.int32)
    local = (position % CPO)[:, None]
    home = (position // CPO)[:, None]
    window = jnp.where(chosen < CPO + local, chosen, chosen + 1)
    other = (home + window // CPO - 1 + N_SHARD) % N_SHARD
    by_position = shuffled[other * CPO + window % CPO]
    return jnp.zeros((CLUSTERS, NB), jnp.int32).at[shuffled].set(by_position)


def cluster_rows(key):
    shuffled, owner_table = placement(key)
    reader_devices = ROWS // ROWS_DEV
    picked = min(ROWS_DEV // 2, N_SHARD // 2)
    per_owner = ROWS_DEV // picked
    weight_factor = jax.random.randint(jax.random.fold_in(key, 103), (N_SHARD,), 1, 5)
    selected_best = jax.random.randint(jax.random.fold_in(key, 104), (), 0, N_SHARD)
    extra_credit = jnp.where(jnp.arange(N_SHARD) == selected_best, 2 ** 21, 0)
    rank_order = jax.random.randint(jax.random.fold_in(key, 105), (reader_devices, N_SHARD), 0, 2 ** 18) * weight_factor[None, :] + extra_credit[None, :]
    rank_order = rank_order * N_SHARD + jnp.arange(N_SHARD)[None, :]
    holder_devices = lax.top_k(rank_order, picked)[1].astype(jnp.int32)
    holder_devices = jnp.repeat(holder_devices, per_owner, axis=1)
    local = jax.random.randint(jax.random.fold_in(key, 106), (reader_devices, ROWS_DEV), 0, CPO)
    members = shuffled[holder_devices * CPO + local]
    shuffle_keys = jax.random.split(jax.random.fold_in(key, 107), reader_devices)
    mixing = jax.vmap(lambda k: jax.random.permutation(k, ROWS_DEV))(shuffle_keys)
    return jnp.take_along_axis(members, mixing, axis=1).reshape(ROWS).astype(jnp.int32)


def draw_clusters(key, part):
    members = cluster_rows(key)
    return members


def draw_owner_map(key, part):
    shuffled, owner_table = placement(key)
    return owner_table


def draw_neighbours(key, part):
    return neighbour_lists(key)


def draw_embeds(key, part):
    members = cluster_rows(key)
    listed = neighbour_lists(key)
    key = jax.random.fold_in(key, 4)
    centres = jax.random.truncated_normal(jax.random.fold_in(key, 1), -5.0, 5.0, (CLUSTERS, D), jnp.float32)
    column = jax.random.randint(jax.random.fold_in(key, 2), (ROWS,), 0, NB)
    other = listed[members, column]
    noise = jax.random.truncated_normal(jax.random.fold_in(key, 3), -5.0, 5.0, (ROWS, D), jnp.float32)
    own_weight = jnp.exp(jax.random.uniform(jax.random.fold_in(key, 5), (ROWS, 1), jnp.float32, -1.2, 0.69))
    side_weight = jnp.exp(jax.random.uniform(jax.random.fold_in(key, 6), (ROWS, 1), jnp.float32, -2.3, 0.18))
    mixed = own_weight * centres[members] + side_weight * centres[other] + noise
    return mixed.astype(jnp.bfloat16)


def setup_inputs(seed: int = 0) -> dict:
    keys = jax.random.split(jax.random.key(seed), 6)
    return {
        "embeds": draw_embeds(jax.random.fold_in(keys[5], 71), 0),
        "clusters": draw_clusters(jax.random.fold_in(keys[5], 71), 0),
        "orders": jax.random.permutation(keys[2], ROWS).astype(jnp.int32),
        "owner_map": draw_owner_map(jax.random.fold_in(keys[5], 71), 0),
        "neighbours": draw_neighbours(jax.random.fold_in(keys[5], 71), 0),
    }


def unit_of(embedded):
    scaled = embedded.astype(jnp.float32)
    mean_square = lax.optimization_barrier(jnp.mean(scaled * scaled, axis=-1, keepdims=True))
    factor = lax.rsqrt(mean_square + 1e-06) * scaled.shape[-1] ** (-0.5)
    return (scaled * factor).astype(jnp.bfloat16)

def reference(embeds, clusters, orders, owner_map, neighbours):
    unit_rows = unit_of(embeds)
    holder_devices = owner_map[clusters].astype(jnp.int32)
    by_owner = jnp.argsort(holder_devices, stable=True).astype(jnp.int32)
    marks = (holder_devices[None, :] == jnp.arange(N_SHARD, dtype=jnp.int32)[:, None]).astype(jnp.int32)
    counts = lax.optimization_barrier(jnp.sum(marks, axis=1)).astype(jnp.int32)
    starts = (jnp.cumsum(counts) - counts).astype(jnp.int32)
    capacity = N_SHARD * N_REP * SLOT
    steps_in = jnp.arange(capacity, dtype=jnp.int32)

    def rows_of(owner_id):
        positions = starts[owner_id] + steps_in
        present = steps_in < counts[owner_id]
        picked = by_owner[jnp.clip(positions, 0, ROWS - 1)].astype(jnp.int32)
        return (picked, present)

    def one_owner(owner_id):
        query_index, query_present = rows_of(owner_id)
        lower_index, lower_present = rows_of((owner_id + N_SHARD - 1) % N_SHARD)
        upper_index, upper_present = rows_of((owner_id + 1) % N_SHARD)
        key_index = jnp.concatenate([lower_index, query_index, upper_index]).astype(jnp.int32)
        key_present = jnp.concatenate([lower_present, query_present, upper_present])
        scores = jnp.dot(unit_rows[query_index], unit_rows[key_index].T, preferred_element_type=jnp.float32)
        query_cluster = clusters[query_index]
        key_cluster = clusters[key_index]
        related = key_cluster[None, :] == query_cluster[:, None]
        listed = neighbours[query_cluster]
        for column in range(NB):
            related = related | (key_cluster[None, :] == listed[:, column][:, None])
        allowed = related & key_present[None, :] & (orders[key_index][None, :] < orders[query_index][:, None])
        best = lax.optimization_barrier(jnp.max(jnp.where(allowed, scores, jnp.float32(-1.0)), axis=1))
        target = jnp.where(query_present, query_index, ROWS).astype(jnp.int32)
        return (target, best)
    targets, values = lax.map(one_owner, jnp.arange(N_SHARD, dtype=jnp.int32))
    result = jnp.full((ROWS,), -1.0, jnp.float32)
    return result.at[targets.reshape(-1)].set(values.reshape(-1).astype(jnp.float32), mode='drop')
```

```python
import jax
import jax.numpy as jnp
from jax import lax
from jax.experimental import pallas as pl
from jax.experimental.pallas import tpu as pltpu
from jax.sharding import PartitionSpec as P

AXES = ("shard", "rep")
Y, Z, X = 8, 8, 4
OWNERS = 128
LOAD = 128
D = 1024
LANES = 128
BLOCKS = D // LANES
ROWS_MSG = 24
WIDE = D + LANES
QUART = 2 * OWNERS
F32, BF16 = jnp.float32, jnp.bfloat16


def device_of(owner, core, half):
    step, bit = divmod(owner % OWNERS, 2)
    y, z = divmod(step, Z)
    if y % 2:
        z = Z - 1 - z
    pair = bit ^ (step & 1)
    return ((y * Z + z) * 2 + core) * X + 2 * pair + (half ^ pair)


QUARTERS = [(core, half) for core in range(2) for half in range(2)]
GROUPS = [[device_of(o, c, h) for o in range(OWNERS)] for c, h in QUARTERS]
EVERY = [[device_of(o, c, h) for o in range(OWNERS) for c, h in QUARTERS]]


def moves(shift, core, half):
    return [
        (device_of(o, c, h), device_of(o + shift, c ^ core, h ^ half))
        for o in range(OWNERS)
        for c, h in QUARTERS
    ]


X_SWAP = moves(0, 0, 1)
C_SWAP = moves(0, 1, 0)
UP = moves(1, 0, 0)
DOWN = moves(-1, 0, 0)


def iota(shape, dim):
    return lax.broadcasted_iota(jnp.int32, shape, dim)


def nt(a, b):
    return lax.dot_general(a, b, (((1,), (1,)), ((), ())), preferred_element_type=F32)


def ones_where(mask):
    return jnp.where(mask, 1.0, 0.0).astype(BF16)


def pack_kernel(x_ref, cl_ref, ord_ref, map_ref, nbr_ref, out_ref, place_ref, wide_ref):
    clusters = cl_ref[...]
    orders = ord_ref[...]
    count = map_ref.shape[1]
    onehot = ones_where(iota((count, LOAD), 0) == clusters)
    first, second = nbr_ref[0:1, :], nbr_ref[1:2, :]
    row = iota((16, count), 0)
    table = jnp.where(row == 0, map_ref[...], 0)
    for at, value in enumerate((first >> 8, first & 255, second >> 8, second & 255)):
        table = jnp.where(row == 4 + at, value, table)
    looked = jnp.dot(table.astype(F32).astype(BF16), onehot, preferred_element_type=F32)
    owner = looked[0:1, :]
    across = jnp.broadcast_to(owner, (LOAD, LOAD))
    below = across.T
    before = iota((LOAD, LOAD), 0) < iota((LOAD, LOAD), 1)
    rank = jnp.sum(jnp.where((across == below) & before, 1.0, 0.0), axis=0, keepdims=True)
    row = iota((16, LOAD), 0)
    meta = jnp.where(row == 8, 1.0, jnp.where((row >= 4) & (row < 8), looked, 0.0))
    for at, value in enumerate((orders >> 8, orders & 255, clusters >> 8, clusters & 255)):
        meta = jnp.where(row == at, value.astype(F32), meta)
    meta = jnp.concatenate([meta, jnp.zeros((LANES - 16, LOAD), F32)], axis=0).astype(BF16)

    scaled = x_ref[...].astype(F32)
    mean_square = jnp.mean(scaled * scaled, axis=-1, keepdims=True)
    factor = lax.rsqrt(mean_square + 1e-06) * D ** (-0.5)
    unit = (scaled * factor).astype(BF16)

    target = iota((OWNERS, LOAD), 0).astype(F32)
    for k in range(2):
        pick = ones_where((owner == target) & (rank == float(k)))
        rows = jnp.dot(pick, unit, preferred_element_type=F32)
        for b in range(BLOCKS):
            at = pl.ds(k * BLOCKS + b, OWNERS, stride=ROWS_MSG)
            wide_ref[at, :] = rows[:, b * LANES : (b + 1) * LANES]
        wide_ref[pl.ds(2 * BLOCKS + k, OWNERS, stride=ROWS_MSG), :] = nt(pick, meta)
    for j in range(2 * BLOCKS + 2, ROWS_MSG):
        wide_ref[pl.ds(j, OWNERS, stride=ROWS_MSG), :] = jnp.zeros((OWNERS, LANES), F32)
    out_ref[...] = wide_ref[...].astype(BF16)
    row = iota((8, LOAD), 0)
    place_ref[...] = jnp.where(row == 0, owner, rank)


def unpack_kernel(got_ref, out_ref, wide_ref):
    wide_ref[...] = got_ref[...].astype(F32)
    for k in range(2):
        here = pl.ds(k * OWNERS, OWNERS)
        for b in range(BLOCKS):
            at = pl.ds(k * BLOCKS + b, OWNERS, stride=ROWS_MSG)
            out_ref[here, pl.ds(b * LANES, LANES)] = wide_ref[at, :].astype(BF16)
        at = pl.ds(2 * BLOCKS + k, OWNERS, stride=ROWS_MSG)
        out_ref[here, pl.ds(D, LANES)] = wide_ref[at, :].astype(BF16)


def key_meta(key_ref):
    row, lane = iota((16, LANES), 0), iota((16, LANES), 1)
    take = jnp.where(lane == 2 * row, 256.0, jnp.where(lane == 2 * row + 1, 1.0, 0.0))
    take = jnp.where(row < 4, take, jnp.where((row == 4) & (lane == 8), 1.0, 0.0))
    got = nt(take.astype(BF16), key_ref[:, D:WIDE])
    order = jnp.where(got[4:5, :] > 0.0, got[0:1, :], 1e9)
    return order, got[1:2, :]


def score_kernel(own_ref, far_ref, core_ref, both_ref, low_ref, high_ref, out_ref):
    device = lax.axis_index("shard") * X + lax.axis_index("rep")
    x = device & 3
    quarter = ((device >> 2) & 1) * 2 + ((x >> 1) ^ (x & 1))
    keys = [(ref, *key_meta(ref)) for ref in (low_ref, own_ref, high_ref)]
    lane = iota((OWNERS, LANES), 1)
    for flip, query in enumerate((own_ref, far_ref, core_ref, both_ref)):
        meta = query[:, D:WIDE].astype(F32)
        order, cluster, first, second = (
            meta[:, 2 * j : 2 * j + 1] * 256.0 + meta[:, 2 * j + 1 : 2 * j + 2] for j in range(4)
        )
        best = None
        for key, key_order, key_cluster in keys:
            scores = nt(query[:, 0:D], key[:, 0:D])
            related = (key_cluster == cluster) | (key_cluster == first) | (key_cluster == second)
            allowed = related & (key_order < order)
            scores = jnp.where(allowed, scores, -1.0)
            best = scores if best is None else jnp.maximum(best, scores)
        best = jnp.max(best, axis=1, keepdims=True)
        pair = jnp.where(lane == 0, best[0:OWNERS, :], best[OWNERS:QUART, :])
        out_ref[pl.ds(quarter ^ flip, OWNERS, stride=4), :] = pair


def pick_kernel(got_ref, place_ref, out_ref):
    best = got_ref[pl.ds(0, OWNERS, stride=4), :]
    for q in range(1, 4):
        best = jnp.maximum(best, got_ref[pl.ds(q, OWNERS, stride=4), :])
    owner, rank = place_ref[0:1, :], place_ref[1:2, :]
    mine = owner == iota((OWNERS, LOAD), 0).astype(F32)
    values = jnp.where(rank == 0.0, best[:, 0:1], best[:, 1:2])
    out_ref[...] = jnp.max(jnp.where(mine, values, -2.0), axis=0, keepdims=True)


def call(kernel, outs, scratch=(), flops=0, size=1 << 20):
    return pl.pallas_call(
        kernel,
        out_shape=outs,
        scratch_shapes=list(scratch),
        compiler_params=pltpu.CompilerParams(vmem_limit_bytes=24 << 20),
        cost_estimate=pl.CostEstimate(flops=flops, bytes_accessed=size, transcendentals=0),
    )


def shape(dims, dtype):
    return jax.ShapeDtypeStruct(dims, dtype)


def body(embeds, clusters, orders, owner_map, neighbours):
    wire = OWNERS * ROWS_MSG
    scratch = [pltpu.VMEM((wire, LANES), F32)]
    packed, place = call(
        pack_kernel, [shape((wire, LANES), BF16), shape((8, LOAD), F32)], scratch, 10**8
    )(
        embeds,
        clusters.reshape(1, LOAD),
        orders.reshape(1, LOAD),
        owner_map.reshape(1, -1),
        neighbours.T,
    )
    got = lax.all_to_all(
        packed.reshape(OWNERS, ROWS_MSG, LANES),
        AXES,
        0,
        0,
        axis_index_groups=GROUPS,
        tiled=True,
    )
    own = call(unpack_kernel, shape((QUART, WIDE), BF16), scratch)(got.reshape(wire, LANES))
    far = lax.ppermute(own, AXES, X_SWAP)
    low = lax.ppermute(own, AXES, UP)
    high = lax.ppermute(own, AXES, DOWN)
    core = lax.ppermute(own, AXES, C_SWAP)
    both = lax.ppermute(far, AXES, C_SWAP)
    best = call(score_kernel, shape((4 * OWNERS, LANES), F32), (), 16 * 10**8)(
        own, far, core, both, low, high
    )
    back = lax.all_to_all(
        best.reshape(4 * OWNERS, 1, LANES), AXES, 0, 0, axis_index_groups=EVERY, tiled=True
    )
    return call(pick_kernel, shape((1, LOAD), F32))(
        back.reshape(4 * OWNERS, LANES), place
    ).reshape(LOAD)


def solution(mesh):
    placed = (P(AXES, None), P(AXES), P(AXES), P(), P())
    return jax.shard_map(body, mesh=mesh, in_specs=placed, out_specs=P(AXES), check_vma=False)
```

```python
import jax
import jax.numpy as jnp
from jax import lax
from jax.experimental import pallas as pl
from jax.experimental.pallas import tpu as pltpu
from jax.sharding import PartitionSpec as P

AXES = ("shard", "rep")
Y, Z, X = 8, 8, 4
OWNERS = 128
LOAD = 128
D = 1024
LANES = 128
WIDE = D + LANES
QUART = 2 * OWNERS
F32, BF16 = jnp.float32, jnp.bfloat16


def device_of(owner, core, half):
    step, bit = divmod(owner % OWNERS, 2)
    y, z = divmod(step, Z)
    if y % 2:
        z = Z - 1 - z
    pair = bit ^ (step & 1)
    return ((y * Z + z) * 2 + core) * X + 2 * pair + (half ^ pair)


QUARTERS = [(core, half) for core in range(2) for half in range(2)]
GROUPS = [[device_of(o, c, h) for o in range(OWNERS)] for c, h in QUARTERS]
EVERY = [[device_of(o, c, h) for o in range(OWNERS) for c, h in QUARTERS]]


def moves(shift, core, half):
    return [
        (device_of(o, c, h), device_of(o + shift, c ^ core, h ^ half))
        for o in range(OWNERS)
        for c, h in QUARTERS
    ]


X_SWAP = moves(0, 0, 1)
C_SWAP = moves(0, 1, 0)
UP = moves(1, 0, 0)
DOWN = moves(-1, 0, 0)


def iota(shape, dim):
    return lax.broadcasted_iota(jnp.int32, shape, dim)


def nt(a, b):
    return lax.dot_general(a, b, (((1,), (1,)), ((), ())), preferred_element_type=F32)


def ones_where(mask):
    return jnp.where(mask, 1.0, 0.0).astype(BF16)


def pack_kernel(x_ref, cl_ref, ord_ref, map_ref, nbr_ref, out_ref, place_ref):
    clusters = cl_ref[...]
    orders = ord_ref[...]
    count = map_ref.shape[1]
    onehot = ones_where(iota((count, LOAD), 0) == clusters)
    first, second = nbr_ref[0:1, :], nbr_ref[1:2, :]
    row = iota((16, count), 0)
    table = jnp.where(row == 0, map_ref[...], 0)
    for at, value in enumerate((first >> 8, first & 255, second >> 8, second & 255)):
        table = jnp.where(row == 4 + at, value, table)
    looked = jnp.dot(table.astype(F32).astype(BF16), onehot, preferred_element_type=F32)
    owner = looked[0:1, :]
    across = jnp.broadcast_to(owner, (LOAD, LOAD))
    below = across.T
    before = iota((LOAD, LOAD), 0) < iota((LOAD, LOAD), 1)
    rank = jnp.sum(jnp.where((across == below) & before, 1.0, 0.0), axis=0, keepdims=True)
    row = iota((16, LOAD), 0)
    meta = jnp.where(row == 8, 1.0, jnp.where((row >= 4) & (row < 8), looked, 0.0))
    for at, value in enumerate((orders >> 8, orders & 255, clusters >> 8, clusters & 255)):
        meta = jnp.where(row == at, value.astype(F32), meta)
    meta = jnp.concatenate([meta, jnp.zeros((LANES - 16, LOAD), F32)], axis=0).astype(BF16)

    scaled = x_ref[...].astype(F32)
    mean_square = jnp.mean(scaled * scaled, axis=-1, keepdims=True)
    factor = lax.rsqrt(mean_square + 1e-06) * D ** (-0.5)
    unit = (scaled * factor).astype(BF16)

    slot = iota((QUART, LOAD), 0)
    pick = (owner == (slot >> 1).astype(F32)) & (rank == (slot & 1).astype(F32))
    pick = ones_where(pick)
    out_ref[:, 0:D] = jnp.dot(pick, unit, preferred_element_type=F32).astype(BF16)
    out_ref[:, D:WIDE] = nt(pick, meta).astype(BF16)
    row = iota((8, LOAD), 0)
    place_ref[...] = jnp.where(row == 0, owner, rank)


def key_meta(key_ref):
    row, lane = iota((16, LANES), 0), iota((16, LANES), 1)
    take = jnp.where(lane == 2 * row, 256.0, jnp.where(lane == 2 * row + 1, 1.0, 0.0))
    take = jnp.where(row < 4, take, jnp.where((row == 4) & (lane == 8), 1.0, 0.0))
    got = nt(take.astype(BF16), key_ref[:, D:WIDE])
    order = jnp.where(got[4:5, :] > 0.0, got[0:1, :], 1e9)
    return order, got[1:2, :]


def score_kernel(own_ref, far_ref, core_ref, both_ref, low_ref, high_ref, out_ref, turn_ref):
    device = lax.axis_index("shard") * X + lax.axis_index("rep")
    x = device & 3
    quarter = ((device >> 2) & 1) * 2 + ((x >> 1) ^ (x & 1))
    keys = [(ref, *key_meta(ref)) for ref in (low_ref, own_ref, high_ref)]
    lane = iota((OWNERS, LANES), 1)
    for flip, query in enumerate((own_ref, far_ref, core_ref, both_ref)):
        meta = query[:, D:WIDE].astype(F32)
        order, cluster, first, second = (
            meta[:, 2 * j : 2 * j + 1] * 256.0 + meta[:, 2 * j + 1 : 2 * j + 2] for j in range(4)
        )
        best = None
        for key, key_order, key_cluster in keys:
            scores = nt(query[:, 0:D], key[:, 0:D])
            related = (key_cluster == cluster) | (key_cluster == first) | (key_cluster == second)
            allowed = related & (key_order < order)
            scores = jnp.where(allowed, scores, -1.0)
            best = scores if best is None else jnp.maximum(best, scores)
        best = jnp.max(best, axis=1, keepdims=True)
        turn_ref[...] = jnp.broadcast_to(best, (QUART, LANES))
        even = turn_ref[pl.ds(0, OWNERS, stride=2), :]
        pair = jnp.where(lane == 0, even, turn_ref[pl.ds(1, OWNERS, stride=2), :])
        out_ref[pl.ds(quarter ^ flip, OWNERS, stride=4), :] = pair


def pick_kernel(got_ref, place_ref, out_ref):
    best = got_ref[pl.ds(0, OWNERS, stride=4), :]
    for q in range(1, 4):
        best = jnp.maximum(best, got_ref[pl.ds(q, OWNERS, stride=4), :])
    owner, rank = place_ref[0:1, :], place_ref[1:2, :]
    mine = owner == iota((OWNERS, LOAD), 0).astype(F32)
    values = jnp.where(rank == 0.0, best[:, 0:1], best[:, 1:2])
    out_ref[...] = jnp.max(jnp.where(mine, values, -2.0), axis=0, keepdims=True)


def call(kernel, outs, scratch=(), flops=0, size=1 << 20):
    return pl.pallas_call(
        kernel,
        out_shape=outs,
        scratch_shapes=list(scratch),
        compiler_params=pltpu.CompilerParams(vmem_limit_bytes=24 << 20),
        cost_estimate=pl.CostEstimate(flops=flops, bytes_accessed=size, transcendentals=0),
    )


def shape(dims, dtype):
    return jax.ShapeDtypeStruct(dims, dtype)


def body(embeds, clusters, orders, owner_map, neighbours):
    packed, place = call(
        pack_kernel, [shape((QUART, WIDE), BF16), shape((8, LOAD), F32)], (), 10**8
    )(
        embeds,
        clusters.reshape(1, LOAD),
        orders.reshape(1, LOAD),
        owner_map.reshape(1, -1),
        neighbours.T,
    )
    got = lax.all_to_all(
        packed.reshape(OWNERS, 2, WIDE), AXES, 0, 0, axis_index_groups=GROUPS, tiled=True
    )
    own = got.reshape(QUART, WIDE)
    far = lax.ppermute(own, AXES, X_SWAP)
    low = lax.ppermute(own, AXES, UP)
    high = lax.ppermute(own, AXES, DOWN)
    core = lax.ppermute(own, AXES, C_SWAP)
    both = lax.ppermute(far, AXES, C_SWAP)
    best = call(score_kernel, shape((4 * OWNERS, LANES), F32), [pltpu.VMEM((QUART, LANES), F32)], 16 * 10**8)(
        own, far, core, both, low, high
    )
    back = lax.all_to_all(
        best.reshape(4 * OWNERS, 1, LANES), AXES, 0, 0, axis_index_groups=EVERY, tiled=True
    )
    return call(pick_kernel, shape((1, LOAD), F32))(
        back.reshape(4 * OWNERS, LANES), place
    ).reshape(LOAD)


def solution(mesh):
    placed = (P(AXES, None), P(AXES), P(AXES), P(), P())
    return jax.shard_map(body, mesh=mesh, in_specs=placed, out_specs=P(AXES), check_vma=False)
```

```python
import jax
import jax.numpy as jnp
from jax import lax
from jax.experimental import pallas as pl
from jax.experimental.pallas import tpu as pltpu
from jax.sharding import PartitionSpec as P

AXES = ("shard", "rep")
Y, Z, X = 8, 8, 4
OWNERS = 128
LOAD = 128
D = 1024
LANES = 128
WIDE = D + LANES
QUART = 2 * OWNERS
F32, BF16 = jnp.float32, jnp.bfloat16


def device_of(owner, core, half):
    step, bit = divmod(owner % OWNERS, 2)
    y, z = divmod(step, Z)
    if y % 2:
        z = Z - 1 - z
    pair = bit ^ (step & 1)
    return ((y * Z + z) * 2 + core) * X + 2 * pair + (half ^ pair)


QUARTERS = [(core, half) for core in range(2) for half in range(2)]
GROUPS = [[device_of(o, c, h) for o in range(OWNERS)] for c, h in QUARTERS]
EVERY = [[device_of(o, c, h) for o in range(OWNERS) for c, h in QUARTERS]]


def moves(shift, core, half):
    return [
        (device_of(o, c, h), device_of(o + shift, c ^ core, h ^ half))
        for o in range(OWNERS)
        for c, h in QUARTERS
    ]


X_SWAP = moves(0, 0, 1)
C_SWAP = moves(0, 1, 0)
DOWN = moves(-1, 0, 0)


def iota(shape, dim):
    return lax.broadcasted_iota(jnp.int32, shape, dim)


def nt(a, b):
    return lax.dot_general(a, b, (((1,), (1,)), ((), ())), preferred_element_type=F32)


def ones_where(mask):
    return jnp.where(mask, 1.0, 0.0).astype(BF16)


def pack_kernel(x_ref, cl_ref, ord_ref, map_ref, nbr_ref, out_ref, place_ref):
    clusters = cl_ref[...]
    orders = ord_ref[...]
    count = map_ref.shape[1]
    onehot = ones_where(iota((count, LOAD), 0) == clusters)
    first, second = nbr_ref[0:1, :], nbr_ref[1:2, :]
    row = iota((16, count), 0)
    table = jnp.where(row == 0, map_ref[...], 0)
    for at, value in enumerate((first >> 8, first & 255, second >> 8, second & 255)):
        table = jnp.where(row == 4 + at, value, table)
    looked = jnp.dot(table.astype(F32).astype(BF16), onehot, preferred_element_type=F32)
    owner = looked[0:1, :]
    across = jnp.broadcast_to(owner, (LOAD, LOAD))
    below = across.T
    before = iota((LOAD, LOAD), 0) < iota((LOAD, LOAD), 1)
    rank = jnp.sum(jnp.where((across == below) & before, 1.0, 0.0), axis=0, keepdims=True)
    row = iota((16, LOAD), 0)
    meta = jnp.where(row == 8, 1.0, jnp.where((row >= 4) & (row < 8), looked, 0.0))
    for at, value in enumerate((orders >> 8, orders & 255, clusters >> 8, clusters & 255)):
        meta = jnp.where(row == at, value.astype(F32), meta)
    meta = jnp.concatenate([meta, jnp.zeros((LANES - 16, LOAD), F32)], axis=0).astype(BF16)

    scaled = x_ref[...].astype(F32)
    mean_square = jnp.mean(scaled * scaled, axis=-1, keepdims=True)
    factor = lax.rsqrt(mean_square + 1e-06) * D ** (-0.5)
    unit = (scaled * factor).astype(BF16)

    slot = iota((QUART, LOAD), 0)
    pick = (owner == (slot >> 1).astype(F32)) & (rank == (slot & 1).astype(F32))
    pick = ones_where(pick)
    out_ref[:, 0:D] = jnp.dot(pick, unit, preferred_element_type=F32).astype(BF16)
    out_ref[:, D:WIDE] = nt(pick, meta).astype(BF16)
    row = iota((8, LOAD), 0)
    place_ref[...] = jnp.where(row == 0, owner, rank)


def key_meta(key_ref):
    row, lane = iota((16, LANES), 0), iota((16, LANES), 1)
    take = jnp.where(lane == 2 * row, 256.0, jnp.where(lane == 2 * row + 1, 1.0, 0.0))
    take = jnp.where(row < 4, take, jnp.where((row == 4) & (lane == 8), 1.0, 0.0))
    got = nt(take.astype(BF16), key_ref[:, D:WIDE])
    order = jnp.where(got[4:5, :] > 0.0, got[0:1, :], 1e9)
    return order, got[1:2, :], got[2:3, :], got[3:4, :]


def masked(scores, query, key):
    order, cluster, first, second = query
    related = (key[1] == cluster) | (key[1] == first) | (key[1] == second)
    return jnp.where(related & (key[0] < order), scores, -1.0)


def score_kernel(own_ref, far_ref, core_ref, both_ref, high_ref, out_ref, turn_ref, top_ref):
    device = lax.axis_index("shard") * X + lax.axis_index("rep")
    x = device & 3
    quarter = ((device >> 2) & 1) * 2 + ((x >> 1) ^ (x & 1))
    own_key, high_key = key_meta(own_ref), key_meta(high_ref)
    lane = iota((OWNERS, LANES), 1)

    def halves(ref):
        return ref[pl.ds(0, OWNERS, stride=2), :], ref[pl.ds(1, OWNERS, stride=2), :]

    upper = None
    for flip, query in ((3, both_ref), (2, core_ref), (1, far_ref), (0, own_ref)):
        digits = query[:, D:WIDE].astype(F32)
        order, cluster, first, second = (
            digits[:, 2 * j : 2 * j + 1] * 256.0 + digits[:, 2 * j + 1 : 2 * j + 2]
            for j in range(4)
        )
        order = jnp.where(digits[:, 8:9] > 0.0, order, 1e9)
        meta = (order, cluster, first, second)
        rows = query[:, 0:D]
        best = masked(nt(rows, own_ref[:, 0:D]), meta, own_key)
        scores = nt(rows, high_ref[:, 0:D])
        best = jnp.maximum(best, masked(scores, meta, high_key))
        best = jnp.max(best, axis=1, keepdims=True)
        over = jnp.max(masked(scores, high_key, meta), axis=0, keepdims=True)
        upper = over if upper is None else jnp.maximum(upper, over)
        turn_ref[...] = jnp.broadcast_to(best, (QUART, LANES))
        even, odd = halves(turn_ref)
        pair = jnp.where(lane == 0, even, jnp.where(lane == 1, odd, -1.0))
        if flip == 0:
            top_ref[...] = jnp.broadcast_to(upper, (LANES, QUART)).T
            even, odd = halves(top_ref)
            pair = jnp.where(lane == 2, even, jnp.where(lane == 3, odd, pair))
        out_ref[pl.ds(quarter ^ flip, OWNERS, stride=4), :] = pair


def pick_kernel(got_ref, place_ref, out_ref):
    best = got_ref[pl.ds(0, OWNERS, stride=4), :]
    for q in range(1, 4):
        best = jnp.maximum(best, got_ref[pl.ds(q, OWNERS, stride=4), :])
    owner, rank = place_ref[0:1, :], place_ref[1:2, :]
    mine = owner == iota((OWNERS, LOAD), 0).astype(F32)
    lower = pltpu.roll(best, 1, 0)
    values = jnp.where(
        rank == 0.0,
        jnp.maximum(best[:, 0:1], lower[:, 2:3]),
        jnp.maximum(best[:, 1:2], lower[:, 3:4]),
    )
    out_ref[...] = jnp.max(jnp.where(mine, values, -2.0), axis=0, keepdims=True)


def call(kernel, outs, scratch=(), flops=0, size=1 << 20):
    return pl.pallas_call(
        kernel,
        out_shape=outs,
        scratch_shapes=list(scratch),
        compiler_params=pltpu.CompilerParams(vmem_limit_bytes=24 << 20),
        cost_estimate=pl.CostEstimate(flops=flops, bytes_accessed=size, transcendentals=0),
    )


def shape(dims, dtype):
    return jax.ShapeDtypeStruct(dims, dtype)


def body(embeds, clusters, orders, owner_map, neighbours):
    packed, place = call(
        pack_kernel, [shape((QUART, WIDE), BF16), shape((8, LOAD), F32)], (), 10**8
    )(
        embeds,
        clusters.reshape(1, LOAD),
        orders.reshape(1, LOAD),
        owner_map.reshape(1, -1),
        neighbours.T,
    )
    got = lax.all_to_all(
        packed.reshape(OWNERS, 2, WIDE), AXES, 0, 0, axis_index_groups=GROUPS, tiled=True
    )
    own = got.reshape(QUART, WIDE)
    far = lax.ppermute(own, AXES, X_SWAP)
    high = lax.ppermute(own, AXES, DOWN)
    core = lax.ppermute(own, AXES, C_SWAP)
    both = lax.ppermute(far, AXES, C_SWAP)
    turn = [pltpu.VMEM((QUART, LANES), F32)] * 2
    best = call(score_kernel, shape((4 * OWNERS, LANES), F32), turn, 11 * 10**8)(
        own, far, core, both, high
    )
    back = lax.all_to_all(
        best.reshape(4 * OWNERS, 1, LANES), AXES, 0, 0, axis_index_groups=EVERY, tiled=True
    )
    return call(pick_kernel, shape((1, LOAD), F32))(
        back.reshape(4 * OWNERS, LANES), place
    ).reshape(LOAD)


def solution(mesh):
    placed = (P(AXES, None), P(AXES), P(AXES), P(), P())
    return jax.shard_map(body, mesh=mesh, in_specs=placed, out_specs=P(AXES), check_vma=False)
```

```python
import jax
import jax.numpy as jnp
from jax import lax
from jax.experimental import pallas as pl
from jax.experimental.pallas import tpu as pltpu
from jax.sharding import PartitionSpec as P

AXES = ("shard", "rep")
Y, Z, X = 8, 8, 4
OWNERS = 128
LOAD = 128
D = 1024
LANES = 128
WIDE = D + LANES
QUART = 2 * OWNERS
F32, BF16 = jnp.float32, jnp.bfloat16


def device_of(owner, core, half):
    step, bit = divmod(owner % OWNERS, 2)
    y, z = divmod(step, Z)
    if y % 2:
        z = Z - 1 - z
    pair = bit ^ (step & 1)
    return ((y * Z + z) * 2 + core) * X + 2 * pair + (half ^ pair)


QUARTERS = [(core, half) for core in range(2) for half in range(2)]
GROUPS = [[device_of(o, c, h) for o in range(OWNERS)] for c, h in QUARTERS]
EVERY = [[device_of(o, c, h) for o in range(OWNERS) for c, h in QUARTERS]]


def moves(shift, core, half):
    return [
        (device_of(o, c, h), device_of(o + shift, c ^ core, h ^ half))
        for o in range(OWNERS)
        for c, h in QUARTERS
    ]


X_SWAP = moves(0, 0, 1)
C_SWAP = moves(0, 1, 0)
DOWN = moves(-1, 0, 0)


def iota(shape, dim):
    return lax.broadcasted_iota(jnp.int32, shape, dim)


def nt(a, b):
    return lax.dot_general(a, b, (((1,), (1,)), ((), ())), preferred_element_type=F32)


def ones_where(mask):
    return jnp.where(mask, 1.0, 0.0).astype(BF16)


def pack_kernel(x_ref, cl_ref, ord_ref, map_ref, nbr_ref, out_ref, place_ref):
    clusters = cl_ref[...]
    orders = ord_ref[...]
    count = map_ref.shape[1]
    onehot = ones_where(iota((count, LOAD), 0) == clusters)
    first, second = nbr_ref[0:1, :], nbr_ref[1:2, :]
    row = iota((16, count), 0)
    table = jnp.where(row == 0, map_ref[...], 0)
    for at, value in enumerate((first >> 8, first & 255, second >> 8, second & 255)):
        table = jnp.where(row == 4 + at, value, table)
    looked = jnp.dot(table.astype(F32).astype(BF16), onehot, preferred_element_type=F32)
    owner = looked[0:1, :]
    across = jnp.broadcast_to(owner, (LOAD, LOAD))
    below = across.T
    before = iota((LOAD, LOAD), 0) < iota((LOAD, LOAD), 1)
    rank = jnp.sum(jnp.where((across == below) & before, 1.0, 0.0), axis=0, keepdims=True)
    row = iota((16, LOAD), 0)
    meta = jnp.where(row == 8, 1.0, jnp.where((row >= 4) & (row < 8), looked, 0.0))
    for at, value in enumerate((orders >> 8, orders & 255, clusters >> 8, clusters & 255)):
        meta = jnp.where(row == at, value.astype(F32), meta)
    meta = jnp.concatenate([meta, jnp.zeros((LANES - 16, LOAD), F32)], axis=0).astype(BF16)

    scaled = x_ref[...].astype(F32)
    mean_square = jnp.mean(scaled * scaled, axis=-1, keepdims=True)
    factor = lax.rsqrt(mean_square + 1e-06) * D ** (-0.5)
    unit = (scaled * factor).astype(BF16)

    slot = iota((QUART, LOAD), 0)
    pick = (owner == (slot >> 1).astype(F32)) & (rank == (slot & 1).astype(F32))
    pick = ones_where(pick)
    out_ref[:, 0:D] = jnp.dot(pick, unit, preferred_element_type=F32).astype(BF16)
    out_ref[:, D:WIDE] = nt(pick, meta).astype(BF16)
    row = iota((8, LOAD), 0)
    place_ref[...] = jnp.where(row == 0, owner, rank)


def key_meta(key_ref):
    row, lane = iota((16, LANES), 0), iota((16, LANES), 1)
    take = jnp.where(lane == 2 * row, 256.0, jnp.where(lane == 2 * row + 1, 1.0, 0.0))
    take = jnp.where(row < 4, take, jnp.where((row == 4) & (lane == 8), 1.0, 0.0))
    got = nt(take.astype(BF16), key_ref[:, D:WIDE])
    order = jnp.where(got[4:5, :] > 0.0, got[0:1, :], 1e9)
    return order, got[1:2, :], got[2:3, :], got[3:4, :]


def masked(scores, query, key):
    order, cluster, first, second = query
    related = (key[1] == cluster) | (key[1] == first) | (key[1] == second)
    return jnp.where(related & (key[0] < order), scores, -1.0)


def my_quarter():
    device = lax.axis_index("shard") * X + lax.axis_index("rep")
    x = device & 3
    return ((device >> 2) & 1) * 2 + ((x >> 1) ^ (x & 1))


def halves(ref):
    return ref[pl.ds(0, OWNERS, stride=2), :], ref[pl.ds(1, OWNERS, stride=2), :]


def score_part(query, own_ref, own_key, high_ref, high_key, turn_ref):
    digits = query[:, D:WIDE].astype(F32)
    order, cluster, first, second = (
        digits[:, 2 * j : 2 * j + 1] * 256.0 + digits[:, 2 * j + 1 : 2 * j + 2] for j in range(4)
    )
    order = jnp.where(digits[:, 8:9] > 0.0, order, 1e9)
    meta = (order, cluster, first, second)
    rows = query[:, 0:D]
    best = masked(nt(rows, own_ref[:, 0:D]), meta, own_key)
    scores = nt(rows, high_ref[:, 0:D])
    best = jnp.maximum(best, masked(scores, meta, high_key))
    best = jnp.max(best, axis=1, keepdims=True)
    upper = jnp.max(masked(scores, high_key, meta), axis=0, keepdims=True)
    turn_ref[...] = jnp.broadcast_to(best, (QUART, LANES))
    even, odd = halves(turn_ref)
    lane = iota((OWNERS, LANES), 1)
    return jnp.where(lane == 0, even, jnp.where(lane == 1, odd, -1.0)), upper


def early_kernel(own_ref, far_ref, core_ref, high_ref, out_ref, upper_ref, turn_ref):
    own_key, high_key = key_meta(own_ref), key_meta(high_ref)
    upper = None
    for flip, query in enumerate((own_ref, far_ref, core_ref)):
        pair, over = score_part(query, own_ref, own_key, high_ref, high_key, turn_ref)
        out_ref[pl.ds(flip * OWNERS, OWNERS), :] = pair
        upper = over if upper is None else jnp.maximum(upper, over)
    upper_ref[...] = jnp.broadcast_to(upper, (8, QUART))


def late_kernel(
    own_ref, both_ref, high_ref, early_ref, upper_ref, out_ref, turn_ref, top_ref
):
    quarter = my_quarter()
    own_key, high_key = key_meta(own_ref), key_meta(high_ref)
    pair, upper = score_part(both_ref, own_ref, own_key, high_ref, high_key, turn_ref)
    out_ref[pl.ds(quarter ^ 3, OWNERS, stride=4), :] = pair
    for flip in (1, 2):
        out_ref[pl.ds(quarter ^ flip, OWNERS, stride=4), :] = early_ref[
            pl.ds(flip * OWNERS, OWNERS), :
        ]
    upper = jnp.maximum(upper, upper_ref[0:1, :])
    top_ref[...] = jnp.broadcast_to(upper, (LANES, QUART)).T
    even, odd = halves(top_ref)
    lane = iota((OWNERS, LANES), 1)
    pair = early_ref[pl.ds(0, OWNERS), :]
    pair = jnp.where(lane == 2, even, jnp.where(lane == 3, odd, pair))
    out_ref[pl.ds(quarter, OWNERS, stride=4), :] = pair


def pick_kernel(got_ref, place_ref, out_ref):
    best = got_ref[pl.ds(0, OWNERS, stride=4), :]
    for q in range(1, 4):
        best = jnp.maximum(best, got_ref[pl.ds(q, OWNERS, stride=4), :])
    owner, rank = place_ref[0:1, :], place_ref[1:2, :]
    mine = owner == iota((OWNERS, LOAD), 0).astype(F32)
    lower = pltpu.roll(best, 1, 0)
    values = jnp.where(
        rank == 0.0,
        jnp.maximum(best[:, 0:1], lower[:, 2:3]),
        jnp.maximum(best[:, 1:2], lower[:, 3:4]),
    )
    out_ref[...] = jnp.max(jnp.where(mine, values, -2.0), axis=0, keepdims=True)


def call(kernel, outs, scratch=(), flops=0, size=1 << 20):
    return pl.pallas_call(
        kernel,
        out_shape=outs,
        scratch_shapes=list(scratch),
        compiler_params=pltpu.CompilerParams(vmem_limit_bytes=24 << 20),
        cost_estimate=pl.CostEstimate(flops=flops, bytes_accessed=size, transcendentals=0),
    )


def shape(dims, dtype):
    return jax.ShapeDtypeStruct(dims, dtype)


def body(embeds, clusters, orders, owner_map, neighbours):
    packed, place = call(
        pack_kernel, [shape((QUART, WIDE), BF16), shape((8, LOAD), F32)], (), 10**8
    )(
        embeds,
        clusters.reshape(1, LOAD),
        orders.reshape(1, LOAD),
        owner_map.reshape(1, -1),
        neighbours.T,
    )
    got = lax.all_to_all(
        packed.reshape(OWNERS, 2, WIDE), AXES, 0, 0, axis_index_groups=GROUPS, tiled=True
    )
    own = got.reshape(QUART, WIDE)
    far = lax.ppermute(own, AXES, X_SWAP)
    high = lax.ppermute(own, AXES, DOWN)
    core = lax.ppermute(own, AXES, C_SWAP)
    both = lax.ppermute(far, AXES, C_SWAP)
    turn = [pltpu.VMEM((QUART, LANES), F32)] * 2
    early, upper = call(
        early_kernel,
        [shape((3 * OWNERS, LANES), F32), shape((8, QUART), F32)],
        turn[:1],
        8 * 10**8,
    )(own, far, core, high)
    best = call(late_kernel, shape((4 * OWNERS, LANES), F32), turn, 3 * 10**8)(
        own, both, high, early, upper
    )
    back = lax.all_to_all(
        best.reshape(4 * OWNERS, 1, LANES), AXES, 0, 0, axis_index_groups=EVERY, tiled=True
    )
    return call(pick_kernel, shape((1, LOAD), F32))(
        back.reshape(4 * OWNERS, LANES), place
    ).reshape(LOAD)


def solution(mesh):
    placed = (P(AXES, None), P(AXES), P(AXES), P(), P())
    return jax.shard_map(body, mesh=mesh, in_specs=placed, out_specs=P(AXES), check_vma=False)
```

```python
import jax
import jax.numpy as jnp
from jax import lax
from jax.experimental import pallas as pl
from jax.experimental.pallas import tpu as pltpu
from jax.sharding import PartitionSpec as P

AXES = ("shard", "rep")
Y, Z, X = 8, 8, 4
OWNERS = 128
LOAD = 128
D = 1024
LANES = 128
WIDE = D + LANES
QUART = 2 * OWNERS
F32, BF16 = jnp.float32, jnp.bfloat16


def device_of(owner, core, half):
    step, bit = divmod(owner % OWNERS, 2)
    y, z = divmod(step, Z)
    if y % 2:
        z = Z - 1 - z
    pair = bit ^ (step & 1)
    return ((y * Z + z) * 2 + core) * X + 2 * pair + (half ^ pair)


QUARTERS = [(core, half) for core in range(2) for half in range(2)]
GROUPS = [[device_of(o, c, h) for o in range(OWNERS)] for c, h in QUARTERS]
EVERY = [[device_of(o, c, h) for o in range(OWNERS) for c, h in QUARTERS]]


def moves(shift, core, half):
    return [
        (device_of(o, c, h), device_of(o + shift, c ^ core, h ^ half))
        for o in range(OWNERS)
        for c, h in QUARTERS
    ]


X_SWAP = moves(0, 0, 1)
C_SWAP = moves(0, 1, 0)
DOWN = moves(-1, 0, 0)


def iota(shape, dim):
    return lax.broadcasted_iota(jnp.int32, shape, dim)


def nt(a, b):
    return lax.dot_general(a, b, (((1,), (1,)), ((), ())), preferred_element_type=F32)


def ones_where(mask):
    return jnp.where(mask, 1.0, 0.0).astype(BF16)


def pack_kernel(x_ref, cl_ref, ord_ref, map_ref, nbr_ref, out_ref, place_ref):
    clusters = cl_ref[...]
    orders = ord_ref[...]
    count = map_ref.shape[1]
    onehot = ones_where(iota((count, LOAD), 0) == clusters)
    first, second = nbr_ref[0:1, :], nbr_ref[1:2, :]
    row = iota((16, count), 0)
    table = jnp.where(row == 0, map_ref[...], 0)
    for at, value in enumerate((first >> 8, first & 255, second >> 8, second & 255)):
        table = jnp.where(row == 4 + at, value, table)
    looked = jnp.dot(table.astype(F32).astype(BF16), onehot, preferred_element_type=F32)
    owner = looked[0:1, :]
    across = jnp.broadcast_to(owner, (LOAD, LOAD))
    below = across.T
    before = iota((LOAD, LOAD), 0) < iota((LOAD, LOAD), 1)
    rank = jnp.sum(jnp.where((across == below) & before, 1.0, 0.0), axis=0, keepdims=True)
    row = iota((16, LOAD), 0)
    meta = jnp.where(row == 8, 1.0, jnp.where((row >= 4) & (row < 8), looked, 0.0))
    for at, value in enumerate((orders >> 8, orders & 255, clusters >> 8, clusters & 255)):
        meta = jnp.where(row == at, value.astype(F32), meta)
    meta = jnp.concatenate([meta, jnp.zeros((LANES - 16, LOAD), F32)], axis=0).astype(BF16)

    scaled = x_ref[...].astype(F32)
    mean_square = jnp.mean(scaled * scaled, axis=-1, keepdims=True)
    factor = lax.rsqrt(mean_square + 1e-06) * D ** (-0.5)
    unit = (scaled * factor).astype(BF16)

    slot = iota((QUART, LOAD), 0)
    pick = (owner == (slot >> 1).astype(F32)) & (rank == (slot & 1).astype(F32))
    pick = ones_where(pick)
    out_ref[:, 0:D] = jnp.dot(pick, unit, preferred_element_type=F32).astype(BF16)
    out_ref[:, D:WIDE] = nt(pick, meta).astype(BF16)
    row = iota((8, LOAD), 0)
    place_ref[...] = jnp.where(row == 0, owner, rank)


def key_meta(key_ref):
    row, lane = iota((16, LANES), 0), iota((16, LANES), 1)
    take = jnp.where(lane == 2 * row, 256.0, jnp.where(lane == 2 * row + 1, 1.0, 0.0))
    take = jnp.where(row < 4, take, jnp.where((row == 4) & (lane == 8), 1.0, 0.0))
    got = nt(take.astype(BF16), key_ref[:, D:WIDE])
    order = jnp.where(got[4:5, :] > 0.0, got[0:1, :], 1e9)
    return order, got[1:2, :], got[2:3, :], got[3:4, :]


def masked(scores, query, key):
    order, cluster, first, second = query
    related = (key[1] == cluster) | (key[1] == first) | (key[1] == second)
    return jnp.where(related & (key[0] < order), scores, -1.0)


def my_quarter():
    device = lax.axis_index("shard") * X + lax.axis_index("rep")
    x = device & 3
    return ((device >> 2) & 1) * 2 + ((x >> 1) ^ (x & 1))


def halves(ref):
    return ref[pl.ds(0, OWNERS, stride=2), :], ref[pl.ds(1, OWNERS, stride=2), :]


def score_part(query, own_ref, own_key, high_ref, high_key, turn_ref):
    digits = query[:, D:WIDE].astype(F32)
    order, cluster, first, second = (
        digits[:, 2 * j : 2 * j + 1] * 256.0 + digits[:, 2 * j + 1 : 2 * j + 2] for j in range(4)
    )
    order = jnp.where(digits[:, 8:9] > 0.0, order, 1e9)
    meta = (order, cluster, first, second)
    rows = query[:, 0:D]
    best = masked(nt(rows, own_ref[:, 0:D]), meta, own_key)
    scores = nt(rows, high_ref[:, 0:D])
    best = jnp.maximum(best, masked(scores, meta, high_key))
    best = jnp.max(best, axis=1, keepdims=True)
    upper = jnp.max(masked(scores, high_key, meta), axis=0, keepdims=True)
    turn_ref[...] = jnp.broadcast_to(best, (QUART, LANES))
    even, odd = halves(turn_ref)
    lane = iota((OWNERS, LANES), 1)
    return jnp.where(lane == 0, even, jnp.where(lane == 1, odd, -1.0)), upper


def early_kernel(own_ref, far_ref, high_ref, out_ref, upper_ref, turn_ref):
    own_key, high_key = key_meta(own_ref), key_meta(high_ref)
    upper = None
    for flip, query in enumerate((own_ref, far_ref)):
        pair, over = score_part(query, own_ref, own_key, high_ref, high_key, turn_ref)
        out_ref[pl.ds(flip * OWNERS, OWNERS), :] = pair
        upper = over if upper is None else jnp.maximum(upper, over)
    upper_ref[...] = jnp.broadcast_to(upper, (8, QUART))


def late_kernel(
    own_ref, core_ref, both_ref, high_ref, early_ref, upper_ref, out_ref, turn_ref, top_ref
):
    quarter = my_quarter()
    own_key, high_key = key_meta(own_ref), key_meta(high_ref)
    upper = upper_ref[0:1, :]
    for flip, query in ((2, core_ref), (3, both_ref)):
        pair, over = score_part(query, own_ref, own_key, high_ref, high_key, turn_ref)
        out_ref[pl.ds(quarter ^ flip, OWNERS, stride=4), :] = pair
        upper = jnp.maximum(upper, over)
    pair = early_ref[pl.ds(OWNERS, OWNERS), :]
    out_ref[pl.ds(quarter ^ 1, OWNERS, stride=4), :] = pair
    top_ref[...] = jnp.broadcast_to(upper, (LANES, QUART)).T
    even, odd = halves(top_ref)
    lane = iota((OWNERS, LANES), 1)
    pair = early_ref[pl.ds(0, OWNERS), :]
    pair = jnp.where(lane == 2, even, jnp.where(lane == 3, odd, pair))
    out_ref[pl.ds(quarter, OWNERS, stride=4), :] = pair


def pick_kernel(got_ref, place_ref, out_ref):
    best = got_ref[pl.ds(0, OWNERS, stride=4), :]
    for q in range(1, 4):
        best = jnp.maximum(best, got_ref[pl.ds(q, OWNERS, stride=4), :])
    owner, rank = place_ref[0:1, :], place_ref[1:2, :]
    mine = owner == iota((OWNERS, LOAD), 0).astype(F32)
    lower = pltpu.roll(best, 1, 0)
    values = jnp.where(
        rank == 0.0,
        jnp.maximum(best[:, 0:1], lower[:, 2:3]),
        jnp.maximum(best[:, 1:2], lower[:, 3:4]),
    )
    out_ref[...] = jnp.max(jnp.where(mine, values, -2.0), axis=0, keepdims=True)


def call(kernel, outs, scratch=(), flops=0, size=1 << 20):
    return pl.pallas_call(
        kernel,
        out_shape=outs,
        scratch_shapes=list(scratch),
        compiler_params=pltpu.CompilerParams(vmem_limit_bytes=24 << 20),
        cost_estimate=pl.CostEstimate(flops=flops, bytes_accessed=size, transcendentals=0),
    )


def shape(dims, dtype):
    return jax.ShapeDtypeStruct(dims, dtype)


def body(embeds, clusters, orders, owner_map, neighbours):
    packed, place = call(
        pack_kernel, [shape((QUART, WIDE), BF16), shape((8, LOAD), F32)], (), 10**8
    )(
        embeds,
        clusters.reshape(1, LOAD),
        orders.reshape(1, LOAD),
        owner_map.reshape(1, -1),
        neighbours.T,
    )
    got = lax.all_to_all(
        packed.reshape(OWNERS, 2, WIDE), AXES, 0, 0, axis_index_groups=GROUPS, tiled=True
    )
    own = got.reshape(QUART, WIDE)
    far = lax.ppermute(own, AXES, X_SWAP)
    high = lax.ppermute(own, AXES, DOWN)
    core = lax.ppermute(own, AXES, C_SWAP)
    both = lax.ppermute(far, AXES, C_SWAP)
    turn = [pltpu.VMEM((QUART, LANES), F32)] * 2
    early, upper = call(
        early_kernel,
        [shape((2 * OWNERS, LANES), F32), shape((8, QUART), F32)],
        turn[:1],
        6 * 10**8,
    )(own, far, high)
    best = call(late_kernel, shape((4 * OWNERS, LANES), F32), turn, 6 * 10**8)(
        own, core, both, high, early, upper
    )
    back = lax.all_to_all(
        best.reshape(4 * OWNERS, 1, LANES), AXES, 0, 0, axis_index_groups=EVERY, tiled=True
    )
    return call(pick_kernel, shape((1, LOAD), F32))(
        back.reshape(4 * OWNERS, LANES), place
    ).reshape(LOAD)


def solution(mesh):
    placed = (P(AXES, None), P(AXES), P(AXES), P(), P())
    return jax.shard_map(body, mesh=mesh, in_specs=placed, out_specs=P(AXES), check_vma=False)
```

```python
import jax
import jax.numpy as jnp
from jax import lax
from jax.experimental import pallas as pl
from jax.experimental.pallas import tpu as pltpu
from jax.sharding import PartitionSpec as P

AXES = ("shard", "rep")
Y, Z, X = 8, 8, 4
OWNERS = 128
LOAD = 128
D = 1024
LANES = 128
WIDE = D + LANES
QUART = 2 * OWNERS
F32, BF16 = jnp.float32, jnp.bfloat16


def device_of(owner, core, half):
    step, bit = divmod(owner % OWNERS, 2)
    y, z = divmod(step, Z)
    if y % 2:
        z = Z - 1 - z
    pair = bit ^ (step & 1)
    return ((y * Z + z) * 2 + core) * X + 2 * pair + (half ^ pair)


QUARTERS = [(core, half) for core in range(2) for half in range(2)]
GROUPS = [[device_of(o, c, h) for o in range(OWNERS)] for c, h in QUARTERS]
EVERY = [[device_of(o, c, h) for o in range(OWNERS) for c, h in QUARTERS]]


def moves(shift, core, half):
    return [
        (device_of(o, c, h), device_of(o + shift, c ^ core, h ^ half))
        for o in range(OWNERS)
        for c, h in QUARTERS
    ]


X_SWAP = moves(0, 0, 1)
C_SWAP = moves(0, 1, 0)
DOWN = moves(-1, 0, 0)


def iota(shape, dim):
    return lax.broadcasted_iota(jnp.int32, shape, dim)


def nt(a, b):
    return lax.dot_general(a, b, (((1,), (1,)), ((), ())), preferred_element_type=F32)


def ones_where(mask):
    return jnp.where(mask, 1.0, 0.0).astype(BF16)


def pack_kernel(
    x_hbm, cl_hbm, ord_hbm, map_hbm, nbr_hbm, out_ref, place_ref,
    x_ref, cl_ref, ord_ref, map_ref, nbr_ref, sems,
):
    pairs = (
        (cl_hbm, cl_ref),
        (map_hbm, map_ref),
        (nbr_hbm, nbr_ref),
        (ord_hbm, ord_ref),
        (x_hbm, x_ref),
    )
    copies = [pltpu.make_async_copy(a, b, sems.at[j]) for j, (a, b) in enumerate(pairs)]
    for copy in copies[::-1]:
        copy.start()
    for copy in copies[:4]:
        copy.wait()
    clusters = cl_ref[...]
    orders = ord_ref[...]
    count = map_ref.shape[1]
    onehot = ones_where(iota((count, LOAD), 0) == clusters)
    first, second = nbr_ref[0:1, :], nbr_ref[1:2, :]
    row = iota((16, count), 0)
    table = jnp.where(row == 0, map_ref[...], 0)
    for at, value in enumerate((first >> 8, first & 255, second >> 8, second & 255)):
        table = jnp.where(row == 4 + at, value, table)
    looked = jnp.dot(table.astype(F32).astype(BF16), onehot, preferred_element_type=F32)
    owner = looked[0:1, :]
    across = jnp.broadcast_to(owner, (LOAD, LOAD))
    below = across.T
    before = iota((LOAD, LOAD), 0) < iota((LOAD, LOAD), 1)
    rank = jnp.sum(jnp.where((across == below) & before, 1.0, 0.0), axis=0, keepdims=True)
    row = iota((16, LOAD), 0)
    meta = jnp.where(row == 8, 1.0, jnp.where((row >= 4) & (row < 8), looked, 0.0))
    for at, value in enumerate((orders >> 8, orders & 255, clusters >> 8, clusters & 255)):
        meta = jnp.where(row == at, value.astype(F32), meta)
    meta = jnp.concatenate([meta, jnp.zeros((LANES - 16, LOAD), F32)], axis=0).astype(BF16)

    copies[4].wait()
    scaled = x_ref[...].astype(F32)
    mean_square = jnp.mean(scaled * scaled, axis=-1, keepdims=True)
    factor = lax.rsqrt(mean_square + 1e-06) * D ** (-0.5)
    unit = (scaled * factor).astype(BF16)

    slot = iota((QUART, LOAD), 0)
    pick = (owner == (slot >> 1).astype(F32)) & (rank == (slot & 1).astype(F32))
    pick = ones_where(pick)
    out_ref[:, 0:D] = jnp.dot(pick, unit, preferred_element_type=F32).astype(BF16)
    out_ref[:, D:WIDE] = nt(pick, meta).astype(BF16)
    row = iota((8, LOAD), 0)
    place_ref[...] = jnp.where(row == 0, owner, rank)


def key_meta(key_ref):
    row, lane = iota((16, LANES), 0), iota((16, LANES), 1)
    take = jnp.where(lane == 2 * row, 256.0, jnp.where(lane == 2 * row + 1, 1.0, 0.0))
    take = jnp.where(row < 4, take, jnp.where((row == 4) & (lane == 8), 1.0, 0.0))
    got = nt(take.astype(BF16), key_ref[:, D:WIDE])
    order = jnp.where(got[4:5, :] > 0.0, got[0:1, :], 1e9)
    return order, got[1:2, :], got[2:3, :], got[3:4, :]


def masked(scores, query, key):
    order, cluster, first, second = query
    related = (key[1] == cluster) | (key[1] == first) | (key[1] == second)
    return jnp.where(related & (key[0] < order), scores, -1.0)


def my_quarter():
    device = lax.axis_index("shard") * X + lax.axis_index("rep")
    x = device & 3
    return ((device >> 2) & 1) * 2 + ((x >> 1) ^ (x & 1))


def halves(ref):
    return ref[pl.ds(0, OWNERS, stride=2), :], ref[pl.ds(1, OWNERS, stride=2), :]


def score_part(query, own_ref, own_key, high_ref, high_key, turn_ref):
    digits = query[:, D:WIDE].astype(F32)
    order, cluster, first, second = (
        digits[:, 2 * j : 2 * j + 1] * 256.0 + digits[:, 2 * j + 1 : 2 * j + 2] for j in range(4)
    )
    order = jnp.where(digits[:, 8:9] > 0.0, order, 1e9)
    meta = (order, cluster, first, second)
    rows = query[:, 0:D]
    best = masked(nt(rows, own_ref[:, 0:D]), meta, own_key)
    scores = nt(rows, high_ref[:, 0:D])
    best = jnp.maximum(best, masked(scores, meta, high_key))
    best = jnp.max(best, axis=1, keepdims=True)
    upper = jnp.max(masked(scores, high_key, meta), axis=0, keepdims=True)
    turn_ref[...] = jnp.broadcast_to(best, (QUART, LANES))
    even, odd = halves(turn_ref)
    lane = iota((OWNERS, LANES), 1)
    return jnp.where(lane == 0, even, jnp.where(lane == 1, odd, -1.0)), upper


def early_kernel(own_ref, far_ref, high_ref, out_ref, upper_ref, turn_ref):
    own_key, high_key = key_meta(own_ref), key_meta(high_ref)
    upper = None
    for flip, query in enumerate((own_ref, far_ref)):
        pair, over = score_part(query, own_ref, own_key, high_ref, high_key, turn_ref)
        out_ref[pl.ds(flip * OWNERS, OWNERS), :] = pair
        upper = over if upper is None else jnp.maximum(upper, over)
    upper_ref[...] = jnp.broadcast_to(upper, (8, QUART))


def late_kernel(
    own_ref, core_ref, both_ref, high_ref, early_ref, upper_ref, out_ref, turn_ref, top_ref
):
    quarter = my_quarter()
    own_key, high_key = key_meta(own_ref), key_meta(high_ref)
    upper = upper_ref[0:1, :]
    for flip, query in ((2, core_ref), (3, both_ref)):
        pair, over = score_part(query, own_ref, own_key, high_ref, high_key, turn_ref)
        out_ref[pl.ds(quarter ^ flip, OWNERS, stride=4), :] = pair
        upper = jnp.maximum(upper, over)
    pair = early_ref[pl.ds(OWNERS, OWNERS), :]
    out_ref[pl.ds(quarter ^ 1, OWNERS, stride=4), :] = pair
    top_ref[...] = jnp.broadcast_to(upper, (LANES, QUART)).T
    even, odd = halves(top_ref)
    lane = iota((OWNERS, LANES), 1)
    pair = early_ref[pl.ds(0, OWNERS), :]
    pair = jnp.where(lane == 2, even, jnp.where(lane == 3, odd, pair))
    out_ref[pl.ds(quarter, OWNERS, stride=4), :] = pair


def pick_kernel(got_ref, place_ref, out_ref):
    best = got_ref[pl.ds(0, OWNERS, stride=4), :]
    for q in range(1, 4):
        best = jnp.maximum(best, got_ref[pl.ds(q, OWNERS, stride=4), :])
    owner, rank = place_ref[0:1, :], place_ref[1:2, :]
    mine = owner == iota((OWNERS, LOAD), 0).astype(F32)
    lower = pltpu.roll(best, 1, 0)
    values = jnp.where(
        rank == 0.0,
        jnp.maximum(best[:, 0:1], lower[:, 2:3]),
        jnp.maximum(best[:, 1:2], lower[:, 3:4]),
    )
    out_ref[...] = jnp.max(jnp.where(mine, values, -2.0), axis=0, keepdims=True)


def call(kernel, outs, scratch=(), flops=0, size=1 << 20, **more):
    return pl.pallas_call(
        kernel,
        **more,
        out_shape=outs,
        scratch_shapes=list(scratch),
        compiler_params=pltpu.CompilerParams(vmem_limit_bytes=24 << 20),
        cost_estimate=pl.CostEstimate(flops=flops, bytes_accessed=size, transcendentals=0),
    )


def shape(dims, dtype):
    return jax.ShapeDtypeStruct(dims, dtype)


def body(embeds, clusters, orders, owner_map, neighbours):
    held = (
        embeds,
        clusters.reshape(1, LOAD),
        orders.reshape(1, LOAD),
        owner_map.reshape(1, -1),
        neighbours.T,
    )
    packed, place = call(
        pack_kernel,
        [shape((QUART, WIDE), BF16), shape((8, LOAD), F32)],
        [pltpu.VMEM(a.shape, a.dtype) for a in held] + [pltpu.SemaphoreType.DMA((5,))],
        10**8,
        in_specs=[pl.BlockSpec(memory_space=pltpu.HBM)] * 5,
    )(*held)
    got = lax.all_to_all(
        packed.reshape(OWNERS, 2, WIDE), AXES, 0, 0, axis_index_groups=GROUPS, tiled=True
    )
    own = got.reshape(QUART, WIDE)
    far = lax.ppermute(own, AXES, X_SWAP)
    high = lax.ppermute(own, AXES, DOWN)
    core = lax.ppermute(own, AXES, C_SWAP)
    both = lax.ppermute(far, AXES, C_SWAP)
    turn = [pltpu.VMEM((QUART, LANES), F32)] * 2
    early, upper = call(
        early_kernel,
        [shape((2 * OWNERS, LANES), F32), shape((8, QUART), F32)],
        turn[:1],
        6 * 10**8,
    )(own, far, high)
    best = call(late_kernel, shape((4 * OWNERS, LANES), F32), turn, 6 * 10**8)(
        own, core, both, high, early, upper
    )
    back = lax.all_to_all(
        best.reshape(4 * OWNERS, 1, LANES), AXES, 0, 0, axis_index_groups=EVERY, tiled=True
    )
    return call(pick_kernel, shape((1, LOAD), F32))(
        back.reshape(4 * OWNERS, LANES), place
    ).reshape(LOAD)


def solution(mesh):
    placed = (P(AXES, None), P(AXES), P(AXES), P(), P())
    return jax.shard_map(body, mesh=mesh, in_specs=placed, out_specs=P(AXES), check_vma=False)
```

```python
import jax
import jax.numpy as jnp
from jax import lax
from jax.experimental import pallas as pl
from jax.experimental.pallas import tpu as pltpu
from jax.sharding import PartitionSpec as P

AXES = ("shard", "rep")
Y, Z, X = 8, 8, 4
OWNERS = 128
LOAD = 128
D = 1024
LANES = 128
WIDE = D + LANES
QUART = 2 * OWNERS
CHIPS = OWNERS // 2
F32, BF16 = jnp.float32, jnp.bfloat16


def device_of(owner, core, half):
    step, bit = divmod(owner % OWNERS, 2)
    y, z = divmod(step, Z)
    if y % 2:
        z = Z - 1 - z
    pair = bit ^ (step & 1)
    return ((y * Z + z) * 2 + core) * X + 2 * pair + (half ^ pair)


QUARTERS = [(core, half) for core in range(2) for half in range(2)]
GROUPS = [sorted(device_of(o, c, h) for o in range(OWNERS)) for c, h in QUARTERS]


def moves(shift, core, half):
    return [
        (device_of(o, c, h), device_of(o + shift, c ^ core, h ^ half))
        for o in range(OWNERS)
        for c, h in QUARTERS
    ]


X_SWAP = moves(0, 0, 1)
C_SWAP = moves(0, 1, 0)
DOWN = moves(-1, 0, 0)


def rank_of(owner):
    step = owner >> 1
    y = step >> 3
    z = (step & 7) ^ (7 * (y & 1))
    return ((y * Z + z) << 1) | ((owner ^ step) & 1)


def iota(shape, dim):
    return lax.broadcasted_iota(jnp.int32, shape, dim)


def nt(a, b):
    return lax.dot_general(a, b, (((1,), (1,)), ((), ())), preferred_element_type=F32)


def ones_where(mask):
    return jnp.where(mask, 1.0, 0.0).astype(BF16)


def pack_kernel(x_ref, cl_ref, ord_ref, map_ref, nbr_ref, out_ref, place_ref):
    clusters = cl_ref[...]
    orders = ord_ref[...]
    count = map_ref.shape[1]
    onehot = ones_where(iota((count, LOAD), 0) == clusters)
    first, second = nbr_ref[0:1, :], nbr_ref[1:2, :]
    row = iota((16, count), 0)
    owners = map_ref[...]
    table = jnp.where(row == 0, rank_of(owners), 0)
    table = jnp.where(row == 1, rank_of((owners + OWNERS - 1) & (OWNERS - 1)), table)
    for at, value in enumerate((first >> 8, first & 255, second >> 8, second & 255)):
        table = jnp.where(row == 4 + at, value, table)
    looked = jnp.dot(table.astype(F32).astype(BF16), onehot, preferred_element_type=F32)
    owner = looked[0:1, :]
    across = jnp.broadcast_to(owner, (LOAD, LOAD))
    below = across.T
    before = iota((LOAD, LOAD), 0) < iota((LOAD, LOAD), 1)
    rank = jnp.sum(jnp.where((across == below) & before, 1.0, 0.0), axis=0, keepdims=True)
    row = iota((16, LOAD), 0)
    meta = jnp.where(row == 8, 1.0, jnp.where((row >= 4) & (row < 8), looked, 0.0))
    for at, value in enumerate((orders >> 8, orders & 255, clusters >> 8, clusters & 255)):
        meta = jnp.where(row == at, value.astype(F32), meta)
    meta = jnp.concatenate([meta, jnp.zeros((LANES - 16, LOAD), F32)], axis=0).astype(BF16)

    scaled = x_ref[...].astype(F32)
    mean_square = jnp.mean(scaled * scaled, axis=-1, keepdims=True)
    factor = lax.rsqrt(mean_square + 1e-06) * D ** (-0.5)
    unit = (scaled * factor).astype(BF16)

    slot = iota((QUART, LOAD), 0)
    pick = (owner == (slot >> 1).astype(F32)) & (rank == (slot & 1).astype(F32))
    pick = ones_where(pick)
    out_ref[:, 0:D] = jnp.dot(pick, unit, preferred_element_type=F32).astype(BF16)
    out_ref[:, D:WIDE] = nt(pick, meta).astype(BF16)
    row = iota((8, LOAD), 0)
    place_ref[...] = jnp.where(row == 0, owner, jnp.where(row == 1, looked[1:2, :], rank))


def key_meta(key_ref):
    row, lane = iota((16, LANES), 0), iota((16, LANES), 1)
    take = jnp.where(lane == 2 * row, 256.0, jnp.where(lane == 2 * row + 1, 1.0, 0.0))
    take = jnp.where(row < 4, take, jnp.where((row == 4) & (lane == 8), 1.0, 0.0))
    got = nt(take.astype(BF16), key_ref[:, D:WIDE])
    order = jnp.where(got[4:5, :] > 0.0, got[0:1, :], 1e9)
    return order, got[1:2, :], got[2:3, :], got[3:4, :]


def masked(scores, query, key):
    order, cluster, first, second = query
    related = (key[1] == cluster) | (key[1] == first) | (key[1] == second)
    return jnp.where(related & (key[0] < order), scores, -1.0)


def place_rows(out_ref, flip, pairs):
    device = lax.axis_index("shard") * X + lax.axis_index("rep")
    core = ((device >> 2) & 1) ^ (flip >> 1)
    half = ((device >> 1) & 1) ^ (device & 1) ^ (flip & 1)
    for pair, values in enumerate(pairs):
        at = 4 * core + 2 * pair + (half ^ pair)
        out_ref[pl.ds(at, CHIPS, stride=8), :] = values


def lanes_of(ref, first, base):
    lane = iota((CHIPS, LANES), 1)
    out = []
    for pair in range(2):
        even, odd = (ref[pl.ds(2 * pair + k, CHIPS, stride=4), :] for k in range(2))
        rest = base[pair] if base is not None else -1.0
        out.append(jnp.where(lane == first, even, jnp.where(lane == first + 1, odd, rest)))
    return out


def score_part(query, own_ref, own_key, high_ref, high_key, turn_ref):
    digits = query[:, D:WIDE].astype(F32)
    order, cluster, first, second = (
        digits[:, 2 * j : 2 * j + 1] * 256.0 + digits[:, 2 * j + 1 : 2 * j + 2] for j in range(4)
    )
    order = jnp.where(digits[:, 8:9] > 0.0, order, 1e9)
    meta = (order, cluster, first, second)
    rows = query[:, 0:D]
    best = masked(nt(rows, own_ref[:, 0:D]), meta, own_key)
    scores = nt(rows, high_ref[:, 0:D])
    best = jnp.maximum(best, masked(scores, meta, high_key))
    best = jnp.max(best, axis=1, keepdims=True)
    upper = jnp.max(masked(scores, high_key, meta), axis=0, keepdims=True)
    turn_ref[...] = jnp.broadcast_to(best, (QUART, LANES))
    return lanes_of(turn_ref, 0, None), upper


def early_kernel(own_ref, far_ref, high_ref, out_ref, upper_ref, turn_ref):
    own_key, high_key = key_meta(own_ref), key_meta(high_ref)
    upper = None
    for flip, query in enumerate((own_ref, far_ref)):
        pairs, over = score_part(query, own_ref, own_key, high_ref, high_key, turn_ref)
        for pair, values in enumerate(pairs):
            out_ref[pl.ds((2 * flip + pair) * CHIPS, CHIPS), :] = values
        upper = over if upper is None else jnp.maximum(upper, over)
    upper_ref[...] = jnp.broadcast_to(upper, (8, QUART))


def late_kernel(
    own_ref, core_ref, both_ref, high_ref, early_ref, upper_ref, out_ref, turn_ref, top_ref
):
    own_key, high_key = key_meta(own_ref), key_meta(high_ref)
    upper = upper_ref[0:1, :]
    for flip, query in ((2, core_ref), (3, both_ref)):
        pairs, over = score_part(query, own_ref, own_key, high_ref, high_key, turn_ref)
        place_rows(out_ref, flip, pairs)
        upper = jnp.maximum(upper, over)
    own, far = (
        [early_ref[pl.ds((2 * flip + pair) * CHIPS, CHIPS), :] for pair in range(2)]
        for flip in range(2)
    )
    place_rows(out_ref, 1, far)
    top_ref[...] = jnp.broadcast_to(upper, (LANES, QUART)).T
    place_rows(out_ref, 0, lanes_of(top_ref, 2, own))


def pick_kernel(got_ref, place_ref, out_ref):
    owner, lower, rank = place_ref[0:1, :], place_ref[1:2, :], place_ref[2:3, :]
    found = jnp.full((1, LOAD), -1.0, F32)
    for pair in range(2):
        best = None
        for at in (0, 1, 4, 5):
            part = got_ref[pl.ds(2 * pair + at, CHIPS, stride=8), :]
            best = part if best is None else jnp.maximum(best, part)
        here = (iota((CHIPS, LOAD), 0) * 2 + pair).astype(F32)
        for target, lane in ((owner, 0), (lower, 2)):
            values = jnp.where(rank == 0.0, best[:, lane : lane + 1], best[:, lane + 1 : lane + 2])
            values = jnp.where(target == here, values, -1.0)
            found = jnp.maximum(found, jnp.max(values, axis=0, keepdims=True))
    out_ref[...] = found


def call(kernel, outs, scratch=(), flops=0, size=1 << 20):
    return pl.pallas_call(
        kernel,
        out_shape=outs,
        scratch_shapes=list(scratch),
        compiler_params=pltpu.CompilerParams(vmem_limit_bytes=24 << 20),
        cost_estimate=pl.CostEstimate(flops=flops, bytes_accessed=size, transcendentals=0),
    )


def shape(dims, dtype):
    return jax.ShapeDtypeStruct(dims, dtype)


def body(embeds, clusters, orders, owner_map, neighbours):
    packed, place = call(
        pack_kernel, [shape((QUART, WIDE), BF16), shape((8, LOAD), F32)], (), 10**8
    )(
        embeds,
        clusters.reshape(1, LOAD),
        orders.reshape(1, LOAD),
        owner_map.reshape(1, -1),
        neighbours.T,
    )
    got = lax.all_to_all(
        packed.reshape(OWNERS, 2, WIDE), AXES, 0, 0, axis_index_groups=GROUPS, tiled=True
    )
    own = got.reshape(QUART, WIDE)
    far = lax.ppermute(own, AXES, X_SWAP)
    high = lax.ppermute(own, AXES, DOWN)
    core = lax.ppermute(own, AXES, C_SWAP)
    both = lax.ppermute(far, AXES, C_SWAP)
    turn = [pltpu.VMEM((QUART, LANES), F32)] * 2
    early, upper = call(
        early_kernel,
        [shape((2 * OWNERS, LANES), F32), shape((8, QUART), F32)],
        turn[:1],
        6 * 10**8,
    )(own, far, high)
    best = call(late_kernel, shape((4 * OWNERS, LANES), F32), turn, 6 * 10**8)(
        own, core, both, high, early, upper
    )
    back = lax.all_to_all(best.reshape(4 * OWNERS, 1, LANES), AXES, 0, 0, tiled=True)
    return call(pick_kernel, shape((1, LOAD), F32))(
        back.reshape(4 * OWNERS, LANES), place
    ).reshape(LOAD)


def solution(mesh):
    placed = (P(AXES, None), P(AXES), P(AXES), P(), P())
    return jax.shard_map(body, mesh=mesh, in_specs=placed, out_specs=P(AXES), check_vma=False)
```

```python
import jax
import jax.numpy as jnp
from jax import lax
from jax.experimental import pallas as pl
from jax.experimental.pallas import tpu as pltpu
from jax.sharding import PartitionSpec as P

AXES = ("shard", "rep")
Y, Z, X = 8, 8, 4
OWNERS = 128
LOAD = 128
D = 1024
LANES = 128
WIDE = D + LANES
QUART = 2 * OWNERS
F32, BF16 = jnp.float32, jnp.bfloat16


def device_of(owner, core, half):
    step, bit = divmod(owner % OWNERS, 2)
    y, z = divmod(step, Z)
    if y % 2:
        z = Z - 1 - z
    pair = bit ^ (step & 1)
    return ((y * Z + z) * 2 + core) * X + 2 * pair + (half ^ pair)


QUARTERS = [(core, half) for core in range(2) for half in range(2)]
OWNED = [[device_of(o, c, h) for c, h in QUARTERS] for o in range(OWNERS)]
GROUPS = [sorted(device_of(o, c, h) for o in range(OWNERS)) for c, h in QUARTERS]


def moves(shift, core, half):
    return [
        (device_of(o, c, h), device_of(o + shift, c ^ core, h ^ half))
        for o in range(OWNERS)
        for c, h in QUARTERS
    ]


X_SWAP = moves(0, 0, 1)
C_SWAP = moves(0, 1, 0)
DOWN = moves(-1, 0, 0)


def rank_of(owner):
    step = owner >> 1
    y = step >> 3
    z = (step & 7) ^ (7 * (y & 1))
    return ((y * Z + z) << 1) | ((owner ^ step) & 1)


def iota(shape, dim):
    return lax.broadcasted_iota(jnp.int32, shape, dim)


def nt(a, b):
    return lax.dot_general(a, b, (((1,), (1,)), ((), ())), preferred_element_type=F32)


def ones_where(mask):
    return jnp.where(mask, 1.0, 0.0).astype(BF16)


def pack_kernel(x_ref, cl_ref, ord_ref, map_ref, nbr_ref, out_ref, place_ref):
    clusters = cl_ref[...]
    orders = ord_ref[...]
    count = map_ref.shape[1]
    onehot = ones_where(iota((count, LOAD), 0) == clusters)
    first, second = nbr_ref[0:1, :], nbr_ref[1:2, :]
    row = iota((16, count), 0)
    owners = map_ref[...]
    table = jnp.where(row == 0, rank_of(owners), 0)
    table = jnp.where(row == 1, rank_of((owners + OWNERS - 1) & (OWNERS - 1)), table)
    for at, value in enumerate((first >> 8, first & 255, second >> 8, second & 255)):
        table = jnp.where(row == 4 + at, value, table)
    looked = jnp.dot(table.astype(F32).astype(BF16), onehot, preferred_element_type=F32)
    owner = looked[0:1, :]
    across = jnp.broadcast_to(owner, (LOAD, LOAD))
    below = across.T
    before = iota((LOAD, LOAD), 0) < iota((LOAD, LOAD), 1)
    rank = jnp.sum(jnp.where((across == below) & before, 1.0, 0.0), axis=0, keepdims=True)
    row = iota((16, LOAD), 0)
    meta = jnp.where(row == 8, 1.0, jnp.where((row >= 4) & (row < 8), looked, 0.0))
    for at, value in enumerate((orders >> 8, orders & 255, clusters >> 8, clusters & 255)):
        meta = jnp.where(row == at, value.astype(F32), meta)
    meta = jnp.concatenate([meta, jnp.zeros((LANES - 16, LOAD), F32)], axis=0).astype(BF16)

    scaled = x_ref[...].astype(F32)
    mean_square = jnp.mean(scaled * scaled, axis=-1, keepdims=True)
    factor = lax.rsqrt(mean_square + 1e-06) * D ** (-0.5)
    unit = (scaled * factor).astype(BF16)

    slot = iota((QUART, LOAD), 0)
    pick = (owner == (slot >> 1).astype(F32)) & (rank == (slot & 1).astype(F32))
    pick = ones_where(pick)
    out_ref[:, 0:D] = jnp.dot(pick, unit, preferred_element_type=F32).astype(BF16)
    out_ref[:, D:WIDE] = nt(pick, meta).astype(BF16)
    row = iota((8, LOAD), 0)
    place_ref[...] = jnp.where(row == 0, owner, jnp.where(row == 1, looked[1:2, :], rank))


def key_meta(key_ref):
    row, lane = iota((16, LANES), 0), iota((16, LANES), 1)
    take = jnp.where(lane == 2 * row, 256.0, jnp.where(lane == 2 * row + 1, 1.0, 0.0))
    take = jnp.where(row < 4, take, jnp.where((row == 4) & (lane == 8), 1.0, 0.0))
    got = nt(take.astype(BF16), key_ref[:, D:WIDE])
    order = jnp.where(got[4:5, :] > 0.0, got[0:1, :], 1e9)
    return order, got[1:2, :], got[2:3, :], got[3:4, :]


def masked(scores, query, key):
    order, cluster, first, second = query
    related = (key[1] == cluster) | (key[1] == first) | (key[1] == second)
    return jnp.where(related & (key[0] < order), scores, -1.0)


def into_lanes(ref, first, base):
    lane = iota((OWNERS, LANES), 1)
    even, odd = (ref[pl.ds(k, OWNERS, stride=2), :] for k in range(2))
    return jnp.where(lane == first, even, jnp.where(lane == first + 1, odd, base))


def score_part(query, own_ref, own_key, high_ref, high_key, turn_ref):
    digits = query[:, D:WIDE].astype(F32)
    order, cluster, first, second = (
        digits[:, 2 * j : 2 * j + 1] * 256.0 + digits[:, 2 * j + 1 : 2 * j + 2] for j in range(4)
    )
    order = jnp.where(digits[:, 8:9] > 0.0, order, 1e9)
    meta = (order, cluster, first, second)
    rows = query[:, 0:D]
    best = masked(nt(rows, own_ref[:, 0:D]), meta, own_key)
    scores = nt(rows, high_ref[:, 0:D])
    best = jnp.maximum(best, masked(scores, meta, high_key))
    best = jnp.max(best, axis=1, keepdims=True)
    upper = jnp.max(masked(scores, high_key, meta), axis=0, keepdims=True)
    turn_ref[...] = jnp.broadcast_to(best, (QUART, LANES))
    return upper


def early_kernel(own_ref, far_ref, high_ref, out_ref, upper_ref, turn_ref):
    own_key, high_key = key_meta(own_ref), key_meta(high_ref)
    upper, found = None, -1.0
    for flip, query in enumerate((own_ref, far_ref)):
        over = score_part(query, own_ref, own_key, high_ref, high_key, turn_ref)
        found = into_lanes(turn_ref, 2 * flip, found)
        upper = over if upper is None else jnp.maximum(upper, over)
    out_ref[...] = found
    upper_ref[...] = jnp.broadcast_to(upper, (8, QUART))


def late_kernel(
    own_ref, core_ref, both_ref, high_ref, early_ref, over_ref, out_ref, upper_ref, turn_ref
):
    own_key, high_key = key_meta(own_ref), key_meta(high_ref)
    upper, found = over_ref[0:1, :], early_ref[...]
    for flip, query in ((2, core_ref), (3, both_ref)):
        over = score_part(query, own_ref, own_key, high_ref, high_key, turn_ref)
        found = into_lanes(turn_ref, 2 * flip, found)
        upper = jnp.maximum(upper, over)
    turn_ref[...] = jnp.broadcast_to(upper, (LANES, QUART)).T
    rows = into_lanes(turn_ref, 8, found).T
    upper_ref[...] = rows[8:16, :]
    device = lax.axis_index("shard") * X + lax.axis_index("rep")
    mine = ((device >> 2) & 1) * 2 + (((device >> 1) ^ device) & 1)
    for q in range(4):
        part = rows[0:2, :]
        for flip in range(1, 4):
            part = jnp.where((mine ^ q) == flip, rows[2 * flip : 2 * flip + 2, :], part)
        out_ref[pl.ds(8 * q, 8), :] = jnp.concatenate([part] * 4, axis=0)


def merge_kernel(got_ref, upper_ref, out_ref):
    best = got_ref[0:8, :]
    for q in range(1, 4):
        best = jnp.maximum(best, got_ref[pl.ds(8 * q, 8), :])
    rows = jnp.concatenate([best[0:2, :], upper_ref[0:2, :], best[0:4, :]], axis=0)
    out_ref[...] = jnp.concatenate([rows] * (OWNERS // 8), axis=0).T


def pick_kernel(got_ref, place_ref, out_ref):
    owner, lower, rank = place_ref[0:1, :], place_ref[1:2, :], place_ref[2:3, :]
    here = iota((OWNERS, LOAD), 0).astype(F32)
    best = got_ref[...]
    found = jnp.full((OWNERS, LOAD), -1.0, F32)
    for target, lane in ((owner, 0), (lower, 2)):
        values = jnp.where(rank == 0.0, best[:, lane : lane + 1], best[:, lane + 1 : lane + 2])
        found = jnp.maximum(found, jnp.where(target == here, values, -1.0))
    out_ref[...] = jnp.max(found, axis=0, keepdims=True)


def call(kernel, outs, scratch=(), flops=0, size=1 << 20):
    return pl.pallas_call(
        kernel,
        out_shape=outs,
        scratch_shapes=list(scratch),
        compiler_params=pltpu.CompilerParams(vmem_limit_bytes=24 << 20),
        cost_estimate=pl.CostEstimate(flops=flops, bytes_accessed=size, transcendentals=0),
    )


def shape(dims, dtype):
    return jax.ShapeDtypeStruct(dims, dtype)


def body(embeds, clusters, orders, owner_map, neighbours):
    packed, place = call(
        pack_kernel, [shape((QUART, WIDE), BF16), shape((8, LOAD), F32)], (), 10**8
    )(
        embeds,
        clusters.reshape(1, LOAD),
        orders.reshape(1, LOAD),
        owner_map.reshape(1, -1),
        neighbours.T,
    )
    got = lax.all_to_all(
        packed.reshape(OWNERS, 2, WIDE), AXES, 0, 0, axis_index_groups=GROUPS, tiled=True
    )
    own = got.reshape(QUART, WIDE)
    far = lax.ppermute(own, AXES, X_SWAP)
    high = lax.ppermute(own, AXES, DOWN)
    core = lax.ppermute(own, AXES, C_SWAP)
    both = lax.ppermute(far, AXES, C_SWAP)
    turn = [pltpu.VMEM((QUART, LANES), F32)]
    early, over = call(
        early_kernel,
        [shape((OWNERS, LANES), F32), shape((8, QUART), F32)],
        turn,
        6 * 10**8,
    )(own, far, high)
    best, upper = call(
        late_kernel, [shape((32, LANES), F32), shape((8, LANES), F32)], turn, 6 * 10**8
    )(own, core, both, high, early, over)
    met = lax.all_to_all(
        best.reshape(4, 8, LANES), AXES, 0, 0, axis_index_groups=OWNED, tiled=True
    )
    best = call(merge_kernel, shape((OWNERS, LANES), F32))(met.reshape(32, LANES), upper)
    back = lax.all_to_all(
        best.reshape(OWNERS, 1, LANES), AXES, 0, 0, axis_index_groups=GROUPS, tiled=True
    )
    return call(pick_kernel, shape((1, LOAD), F32))(
        back.reshape(OWNERS, LANES), place
    ).reshape(LOAD)


def solution(mesh):
    placed = (P(AXES, None), P(AXES), P(AXES), P(), P())
    return jax.shard_map(body, mesh=mesh, in_specs=placed, out_specs=P(AXES), check_vma=False)
```

```python
import jax
import jax.numpy as jnp
from jax import lax
from jax.experimental import pallas as pl
from jax.experimental.pallas import tpu as pltpu
from jax.sharding import PartitionSpec as P

AXES = ("shard", "rep")
Y, Z, X = 8, 8, 4
OWNERS = 128
LOAD = 128
D = 1024
LANES = 128
WIDE = D + LANES
QUART = 2 * OWNERS
F32, BF16 = jnp.float32, jnp.bfloat16


def device_of(owner, core, half):
    step, bit = divmod(owner % OWNERS, 2)
    y, z = divmod(step, Z)
    if y % 2:
        z = Z - 1 - z
    pair = bit ^ (step & 1)
    return ((y * Z + z) * 2 + core) * X + 2 * pair + (half ^ pair)


QUARTERS = [(core, half) for core in range(2) for half in range(2)]
GROUPS = [
    sorted((device_of(o, c, h) for o in range(OWNERS)), reverse=c == 1) for c, h in QUARTERS
]
EVERY = [[group[at] for at in range(OWNERS) for group in GROUPS]]


def moves(shift, core, half):
    return [
        (device_of(o, c, h), device_of(o + shift, c ^ core, h ^ half))
        for o in range(OWNERS)
        for c, h in QUARTERS
    ]


X_SWAP = moves(0, 0, 1)
C_SWAP = moves(0, 1, 0)
DOWN = moves(-1, 0, 0)


def rank_of(owner):
    step = owner >> 1
    y = step >> 3
    z = (step & 7) ^ (7 * (y & 1))
    return ((y * Z + z) << 1) | ((owner ^ step) & 1)


def iota(shape, dim):
    return lax.broadcasted_iota(jnp.int32, shape, dim)


def nt(a, b):
    return lax.dot_general(a, b, (((1,), (1,)), ((), ())), preferred_element_type=F32)


def ones_where(mask):
    return jnp.where(mask, 1.0, 0.0).astype(BF16)


def pack_kernel(x_ref, cl_ref, ord_ref, map_ref, nbr_ref, out_ref, place_ref):
    clusters = cl_ref[...]
    orders = ord_ref[...]
    count = map_ref.shape[1]
    onehot = ones_where(iota((count, LOAD), 0) == clusters)
    first, second = nbr_ref[0:1, :], nbr_ref[1:2, :]
    row = iota((16, count), 0)
    owners = map_ref[...]
    table = jnp.where(row == 0, rank_of(owners), 0)
    table = jnp.where(row == 1, rank_of((owners + OWNERS - 1) & (OWNERS - 1)), table)
    for at, value in enumerate((first >> 8, first & 255, second >> 8, second & 255)):
        table = jnp.where(row == 4 + at, value, table)
    looked = jnp.dot(table.astype(F32).astype(BF16), onehot, preferred_element_type=F32)
    owner = looked[0:1, :]
    across = jnp.broadcast_to(owner, (LOAD, LOAD))
    below = across.T
    before = iota((LOAD, LOAD), 0) < iota((LOAD, LOAD), 1)
    rank = jnp.sum(jnp.where((across == below) & before, 1.0, 0.0), axis=0, keepdims=True)
    row = iota((16, LOAD), 0)
    meta = jnp.where(row == 8, 1.0, jnp.where((row >= 4) & (row < 8), looked, 0.0))
    for at, value in enumerate((orders >> 8, orders & 255, clusters >> 8, clusters & 255)):
        meta = jnp.where(row == at, value.astype(F32), meta)
    meta = jnp.concatenate([meta, jnp.zeros((LANES - 16, LOAD), F32)], axis=0).astype(BF16)

    scaled = x_ref[...].astype(F32)
    mean_square = jnp.mean(scaled * scaled, axis=-1, keepdims=True)
    factor = lax.rsqrt(mean_square + 1e-06) * D ** (-0.5)
    unit = (scaled * factor).astype(BF16)

    slot = iota((QUART, LOAD), 0)
    target = (slot >> 1) ^ ((lax.axis_index("shard") & 1) * (OWNERS - 1))
    pick = (owner == target.astype(F32)) & (rank == (slot & 1).astype(F32))
    pick = ones_where(pick)
    out_ref[:, 0:D] = jnp.dot(pick, unit, preferred_element_type=F32).astype(BF16)
    out_ref[:, D:WIDE] = nt(pick, meta).astype(BF16)
    row = iota((8, LOAD), 0)
    place_ref[...] = jnp.where(row == 0, owner, jnp.where(row == 1, looked[1:2, :], rank))


def key_meta(key_ref):
    row, lane = iota((16, LANES), 0), iota((16, LANES), 1)
    take = jnp.where(lane == 2 * row, 256.0, jnp.where(lane == 2 * row + 1, 1.0, 0.0))
    take = jnp.where(row < 4, take, jnp.where((row == 4) & (lane == 8), 1.0, 0.0))
    got = nt(take.astype(BF16), key_ref[:, D:WIDE])
    order = jnp.where(got[4:5, :] > 0.0, got[0:1, :], 1e9)
    return order, got[1:2, :], got[2:3, :], got[3:4, :]


def masked(scores, query, key):
    order, cluster, first, second = query
    related = (key[1] == cluster) | (key[1] == first) | (key[1] == second)
    return jnp.where(related & (key[0] < order), scores, -1.0)


def my_quarter():
    device = lax.axis_index("shard") * X + lax.axis_index("rep")
    x = device & 3
    return ((device >> 2) & 1) * 2 + ((x >> 1) ^ (x & 1))


def halves(ref):
    return ref[pl.ds(0, OWNERS, stride=2), :], ref[pl.ds(1, OWNERS, stride=2), :]


def score_part(query, own_ref, own_key, high_ref, high_key, turn_ref):
    digits = query[:, D:WIDE].astype(F32)
    order, cluster, first, second = (
        digits[:, 2 * j : 2 * j + 1] * 256.0 + digits[:, 2 * j + 1 : 2 * j + 2] for j in range(4)
    )
    order = jnp.where(digits[:, 8:9] > 0.0, order, 1e9)
    meta = (order, cluster, first, second)
    rows = query[:, 0:D]
    best = masked(nt(rows, own_ref[:, 0:D]), meta, own_key)
    scores = nt(rows, high_ref[:, 0:D])
    best = jnp.maximum(best, masked(scores, meta, high_key))
    best = jnp.max(best, axis=1, keepdims=True)
    upper = jnp.max(masked(scores, high_key, meta), axis=0, keepdims=True)
    turn_ref[...] = jnp.broadcast_to(best, (QUART, LANES))
    even, odd = halves(turn_ref)
    lane = iota((OWNERS, LANES), 1)
    return jnp.where(lane == 0, even, jnp.where(lane == 1, odd, -1.0)), upper


def early_kernel(own_ref, far_ref, high_ref, out_ref, upper_ref, turn_ref):
    own_key, high_key = key_meta(own_ref), key_meta(high_ref)
    upper = None
    for flip, query in enumerate((own_ref, far_ref)):
        pair, over = score_part(query, own_ref, own_key, high_ref, high_key, turn_ref)
        out_ref[pl.ds(flip * OWNERS, OWNERS), :] = pair
        upper = over if upper is None else jnp.maximum(upper, over)
    upper_ref[...] = jnp.broadcast_to(upper, (8, QUART))


def late_kernel(
    own_ref, core_ref, both_ref, high_ref, early_ref, upper_ref, out_ref, turn_ref, top_ref
):
    quarter = my_quarter()
    own_key, high_key = key_meta(own_ref), key_meta(high_ref)
    upper = upper_ref[0:1, :]
    for flip, query in ((2, core_ref), (3, both_ref)):
        pair, over = score_part(query, own_ref, own_key, high_ref, high_key, turn_ref)
        out_ref[pl.ds(quarter ^ flip, OWNERS, stride=4), :] = pair
        upper = jnp.maximum(upper, over)
    pair = early_ref[pl.ds(OWNERS, OWNERS), :]
    out_ref[pl.ds(quarter ^ 1, OWNERS, stride=4), :] = pair
    top_ref[...] = jnp.broadcast_to(upper, (LANES, QUART)).T
    even, odd = halves(top_ref)
    lane = iota((OWNERS, LANES), 1)
    pair = early_ref[pl.ds(0, OWNERS), :]
    pair = jnp.where(lane == 2, even, jnp.where(lane == 3, odd, pair))
    out_ref[pl.ds(quarter, OWNERS, stride=4), :] = pair


def pick_kernel(got_ref, place_ref, out_ref):
    owner, lower, rank = place_ref[0:1, :], place_ref[1:2, :], place_ref[2:3, :]
    at = iota((OWNERS, LOAD), 0)
    found = jnp.full((OWNERS, LOAD), -1.0, F32)
    for core in range(2):
        best = jnp.maximum(
            got_ref[pl.ds(2 * core, OWNERS, stride=4), :],
            got_ref[pl.ds(2 * core + 1, OWNERS, stride=4), :],
        )
        here = (at ^ (core * (OWNERS - 1))).astype(F32)
        for target, lane in ((owner, 0), (lower, 2)):
            values = jnp.where(rank == 0.0, best[:, lane : lane + 1], best[:, lane + 1 : lane + 2])
            found = jnp.maximum(found, jnp.where(target == here, values, -1.0))
    out_ref[...] = jnp.max(found, axis=0, keepdims=True)


def call(kernel, outs, scratch=(), flops=0, size=1 << 20):
    return pl.pallas_call(
        kernel,
        out_shape=outs,
        scratch_shapes=list(scratch),
        compiler_params=pltpu.CompilerParams(vmem_limit_bytes=24 << 20),
        cost_estimate=pl.CostEstimate(flops=flops, bytes_accessed=size, transcendentals=0),
    )


def shape(dims, dtype):
    return jax.ShapeDtypeStruct(dims, dtype)


def body(embeds, clusters, orders, owner_map, neighbours):
    packed, place = call(
        pack_kernel, [shape((QUART, WIDE), BF16), shape((8, LOAD), F32)], (), 10**8
    )(
        embeds,
        clusters.reshape(1, LOAD),
        orders.reshape(1, LOAD),
        owner_map.reshape(1, -1),
        neighbours.T,
    )
    got = lax.all_to_all(
        packed.reshape(OWNERS, 2, WIDE), AXES, 0, 0, axis_index_groups=GROUPS, tiled=True
    )
    own = got.reshape(QUART, WIDE)
    far = lax.ppermute(own, AXES, X_SWAP)
    high = lax.ppermute(own, AXES, DOWN)
    core = lax.ppermute(own, AXES, C_SWAP)
    both = lax.ppermute(far, AXES, C_SWAP)
    turn = [pltpu.VMEM((QUART, LANES), F32)] * 2
    early, upper = call(
        early_kernel,
        [shape((2 * OWNERS, LANES), F32), shape((8, QUART), F32)],
        turn[:1],
        6 * 10**8,
    )(own, far, high)
    best = call(late_kernel, shape((4 * OWNERS, LANES), F32), turn, 6 * 10**8)(
        own, core, both, high, early, upper
    )
    back = lax.all_to_all(
        best.reshape(4 * OWNERS, 1, LANES), AXES, 0, 0, axis_index_groups=EVERY, tiled=True
    )
    return call(pick_kernel, shape((1, LOAD), F32))(
        back.reshape(4 * OWNERS, LANES), place
    ).reshape(LOAD)


def solution(mesh):
    placed = (P(AXES, None), P(AXES), P(AXES), P(), P())
    return jax.shard_map(body, mesh=mesh, in_specs=placed, out_specs=P(AXES), check_vma=False)
```

```python
import jax
import jax.numpy as jnp
from jax import lax
from jax.experimental import pallas as pl
from jax.experimental.pallas import tpu as pltpu
from jax.sharding import PartitionSpec as P

AXES = ("shard", "rep")
Y, Z, X = 8, 8, 4
OWNERS = 128
LOAD = 128
D = 1024
LANES = 128
WIDE = D + LANES
QUART = 2 * OWNERS
F32, BF16 = jnp.float32, jnp.bfloat16


def device_of(owner, core, half):
    step, bit = divmod(owner % OWNERS, 2)
    y, z = divmod(step, Z)
    if y % 2:
        z = Z - 1 - z
    pair = bit ^ (step & 1)
    return ((y * Z + z) * 2 + core) * X + 2 * pair + (half ^ pair)


QUARTERS = [(core, half) for core in range(2) for half in range(2)]
OWNED = [[device_of(o, c, h) for c, h in QUARTERS] for o in range(OWNERS)]
GROUPS = [
    sorted((device_of(o, c, h) for o in range(OWNERS)), reverse=c == 1) for c, h in QUARTERS
]


def moves(shift, core, half):
    return [
        (device_of(o, c, h), device_of(o + shift, c ^ core, h ^ half))
        for o in range(OWNERS)
        for c, h in QUARTERS
    ]


X_SWAP = moves(0, 0, 1)
C_SWAP = moves(0, 1, 0)
DOWN = moves(-1, 0, 0)


def rank_of(owner):
    step = owner >> 1
    y = step >> 3
    z = (step & 7) ^ (7 * (y & 1))
    return ((y * Z + z) << 1) | ((owner ^ step) & 1)


def turned():
    return (lax.axis_index("shard") & 1) * (OWNERS - 1)


def iota(shape, dim):
    return lax.broadcasted_iota(jnp.int32, shape, dim)


def nt(a, b):
    return lax.dot_general(a, b, (((1,), (1,)), ((), ())), preferred_element_type=F32)


def ones_where(mask):
    return jnp.where(mask, 1.0, 0.0).astype(BF16)


def pack_kernel(x_ref, cl_ref, ord_ref, map_ref, nbr_ref, out_ref, place_ref):
    clusters = cl_ref[...]
    orders = ord_ref[...]
    count = map_ref.shape[1]
    onehot = ones_where(iota((count, LOAD), 0) == clusters)
    first, second = nbr_ref[0:1, :], nbr_ref[1:2, :]
    row = iota((16, count), 0)
    owners = map_ref[...]
    table = jnp.where(row == 0, rank_of(owners), 0)
    table = jnp.where(row == 1, rank_of((owners + OWNERS - 1) & (OWNERS - 1)), table)
    for at, value in enumerate((first >> 8, first & 255, second >> 8, second & 255)):
        table = jnp.where(row == 4 + at, value, table)
    looked = jnp.dot(table.astype(F32).astype(BF16), onehot, preferred_element_type=F32)
    owner = looked[0:1, :]
    across = jnp.broadcast_to(owner, (LOAD, LOAD))
    below = across.T
    before = iota((LOAD, LOAD), 0) < iota((LOAD, LOAD), 1)
    rank = jnp.sum(jnp.where((across == below) & before, 1.0, 0.0), axis=0, keepdims=True)
    row = iota((16, LOAD), 0)
    meta = jnp.where(row == 8, 1.0, jnp.where((row >= 4) & (row < 8), looked, 0.0))
    for at, value in enumerate((orders >> 8, orders & 255, clusters >> 8, clusters & 255)):
        meta = jnp.where(row == at, value.astype(F32), meta)
    meta = jnp.concatenate([meta, jnp.zeros((LANES - 16, LOAD), F32)], axis=0).astype(BF16)

    scaled = x_ref[...].astype(F32)
    mean_square = jnp.mean(scaled * scaled, axis=-1, keepdims=True)
    factor = lax.rsqrt(mean_square + 1e-06) * D ** (-0.5)
    unit = (scaled * factor).astype(BF16)

    slot = iota((QUART, LOAD), 0)
    target = (slot >> 1) ^ turned()
    pick = (owner == target.astype(F32)) & (rank == (slot & 1).astype(F32))
    pick = ones_where(pick)
    out_ref[:, 0:D] = jnp.dot(pick, unit, preferred_element_type=F32).astype(BF16)
    out_ref[:, D:WIDE] = nt(pick, meta).astype(BF16)
    row = iota((8, LOAD), 0)
    place_ref[...] = jnp.where(row == 0, owner, jnp.where(row == 1, looked[1:2, :], rank))


def key_meta(key_ref):
    row, lane = iota((16, LANES), 0), iota((16, LANES), 1)
    take = jnp.where(lane == 2 * row, 256.0, jnp.where(lane == 2 * row + 1, 1.0, 0.0))
    take = jnp.where(row < 4, take, jnp.where((row == 4) & (lane == 8), 1.0, 0.0))
    got = nt(take.astype(BF16), key_ref[:, D:WIDE])
    order = jnp.where(got[4:5, :] > 0.0, got[0:1, :], 1e9)
    return order, got[1:2, :], got[2:3, :], got[3:4, :]


def masked(scores, query, key):
    order, cluster, first, second = query
    related = (key[1] == cluster) | (key[1] == first) | (key[1] == second)
    return jnp.where(related & (key[0] < order), scores, -1.0)


def into_lanes(ref, first, base):
    lane = iota((OWNERS, LANES), 1)
    even, odd = (ref[pl.ds(k, OWNERS, stride=2), :] for k in range(2))
    return jnp.where(lane == first, even, jnp.where(lane == first + 1, odd, base))


def score_part(query, own_ref, own_key, high_ref, high_key, turn_ref):
    digits = query[:, D:WIDE].astype(F32)
    order, cluster, first, second = (
        digits[:, 2 * j : 2 * j + 1] * 256.0 + digits[:, 2 * j + 1 : 2 * j + 2] for j in range(4)
    )
    order = jnp.where(digits[:, 8:9] > 0.0, order, 1e9)
    meta = (order, cluster, first, second)
    rows = query[:, 0:D]
    best = masked(nt(rows, own_ref[:, 0:D]), meta, own_key)
    scores = nt(rows, high_ref[:, 0:D])
    best = jnp.maximum(best, masked(scores, meta, high_key))
    best = jnp.max(best, axis=1, keepdims=True)
    upper = jnp.max(masked(scores, high_key, meta), axis=0, keepdims=True)
    turn_ref[...] = jnp.broadcast_to(best, (QUART, LANES))
    return upper


def early_kernel(own_ref, far_ref, high_ref, out_ref, upper_ref, turn_ref):
    own_key, high_key = key_meta(own_ref), key_meta(high_ref)
    upper, found = None, -1.0
    for flip, query in enumerate((own_ref, far_ref)):
        over = score_part(query, own_ref, own_key, high_ref, high_key, turn_ref)
        found = into_lanes(turn_ref, 2 * flip, found)
        upper = over if upper is None else jnp.maximum(upper, over)
    out_ref[...] = found
    upper_ref[...] = jnp.broadcast_to(upper, (8, QUART))


def late_kernel(
    own_ref, core_ref, both_ref, high_ref, early_ref, over_ref, out_ref, upper_ref, turn_ref
):
    own_key, high_key = key_meta(own_ref), key_meta(high_ref)
    upper, found = over_ref[0:1, :], early_ref[...]
    for flip, query in ((2, core_ref), (3, both_ref)):
        over = score_part(query, own_ref, own_key, high_ref, high_key, turn_ref)
        found = into_lanes(turn_ref, 2 * flip, found)
        upper = jnp.maximum(upper, over)
    turn_ref[...] = jnp.broadcast_to(upper, (LANES, QUART)).T
    rows = into_lanes(turn_ref, 8, found).T
    upper_ref[...] = rows[8:16, :]
    device = lax.axis_index("shard") * X + lax.axis_index("rep")
    mine = ((device >> 2) & 1) * 2 + (((device >> 1) ^ device) & 1)
    for q in range(4):
        part = rows[0:2, :]
        for flip in range(1, 4):
            part = jnp.where((mine ^ q) == flip, rows[2 * flip : 2 * flip + 2, :], part)
        out_ref[pl.ds(8 * q, 8), :] = jnp.concatenate([part] * 4, axis=0)


def merge_kernel(got_ref, upper_ref, out_ref):
    best = got_ref[0:8, :]
    for q in range(1, 4):
        best = jnp.maximum(best, got_ref[pl.ds(8 * q, 8), :])
    rows = jnp.concatenate([best[0:2, :], upper_ref[0:2, :], best[0:4, :]], axis=0)
    out_ref[...] = jnp.concatenate([rows] * (OWNERS // 8), axis=0).T


def pick_kernel(got_ref, place_ref, out_ref):
    owner, lower, rank = place_ref[0:1, :], place_ref[1:2, :], place_ref[2:3, :]
    here = (iota((OWNERS, LOAD), 0) ^ turned()).astype(F32)
    best = got_ref[...]
    found = jnp.full((OWNERS, LOAD), -1.0, F32)
    for target, lane in ((owner, 0), (lower, 2)):
        values = jnp.where(rank == 0.0, best[:, lane : lane + 1], best[:, lane + 1 : lane + 2])
        found = jnp.maximum(found, jnp.where(target == here, values, -1.0))
    out_ref[...] = jnp.max(found, axis=0, keepdims=True)


def call(kernel, outs, scratch=(), flops=0, size=1 << 20):
    return pl.pallas_call(
        kernel,
        out_shape=outs,
        scratch_shapes=list(scratch),
        compiler_params=pltpu.CompilerParams(vmem_limit_bytes=24 << 20),
        cost_estimate=pl.CostEstimate(flops=flops, bytes_accessed=size, transcendentals=0),
    )


def shape(dims, dtype):
    return jax.ShapeDtypeStruct(dims, dtype)


def body(embeds, clusters, orders, owner_map, neighbours):
    packed, place = call(
        pack_kernel, [shape((QUART, WIDE), BF16), shape((8, LOAD), F32)], (), 10**8
    )(
        embeds,
        clusters.reshape(1, LOAD),
        orders.reshape(1, LOAD),
        owner_map.reshape(1, -1),
        neighbours.T,
    )
    got = lax.all_to_all(
        packed.reshape(OWNERS, 2, WIDE), AXES, 0, 0, axis_index_groups=GROUPS, tiled=True
    )
    own = got.reshape(QUART, WIDE)
    far = lax.ppermute(own, AXES, X_SWAP)
    high = lax.ppermute(own, AXES, DOWN)
    core = lax.ppermute(own, AXES, C_SWAP)
    both = lax.ppermute(far, AXES, C_SWAP)
    turn = [pltpu.VMEM((QUART, LANES), F32)]
    early, over = call(
        early_kernel,
        [shape((OWNERS, LANES), F32), shape((8, QUART), F32)],
        turn,
        6 * 10**8,
    )(own, far, high)
    best, upper = call(
        late_kernel, [shape((32, LANES), F32), shape((8, LANES), F32)], turn, 6 * 10**8
    )(own, core, both, high, early, over)
    met = lax.all_to_all(
        best.reshape(4, 8, LANES), AXES, 0, 0, axis_index_groups=OWNED, tiled=True
    )
    best = call(merge_kernel, shape((OWNERS, LANES), F32))(met.reshape(32, LANES), upper)
    back = lax.all_to_all(
        best.reshape(OWNERS, 1, LANES), AXES, 0, 0, axis_index_groups=GROUPS, tiled=True
    )
    return call(pick_kernel, shape((1, LOAD), F32))(
        back.reshape(OWNERS, LANES), place
    ).reshape(LOAD)


def solution(mesh):
    placed = (P(AXES, None), P(AXES), P(AXES), P(), P())
    return jax.shard_map(body, mesh=mesh, in_specs=placed, out_specs=P(AXES), check_vma=False)
```

```python
import jax
import jax.numpy as jnp
from jax import lax
from jax.experimental import pallas as pl
from jax.experimental.pallas import tpu as pltpu
from jax.sharding import PartitionSpec as P

AXES = ("shard", "rep")
Y, Z, X = 8, 8, 4
OWNERS = 128
LOAD = 128
D = 1024
LANES = 128
WIDE = D + LANES
QUART = 2 * OWNERS
F32, BF16 = jnp.float32, jnp.bfloat16


def device_of(owner, core, half):
    step, bit = divmod(owner % OWNERS, 2)
    y, z = divmod(step, Z)
    if y % 2:
        z = Z - 1 - z
    pair = bit ^ (step & 1)
    return ((y * Z + z) * 2 + core) * X + 2 * pair + (half ^ pair)


QUARTERS = [(core, half) for core in range(2) for half in range(2)]
OWNED = [[device_of(o, c, h) for c, h in QUARTERS] for o in range(OWNERS)]


def rank_of(owner, core):
    step = owner >> 1
    y = step >> 3
    z = (step & 7) ^ (7 * (y & 1))
    major, minor = y + core * (z - y), z + core * (y - z)
    return (((major * Z + minor) << 1) | ((owner ^ step) & 1)) ^ (core * (OWNERS - 1))


GROUPS = [
    [device_of(o, c, h) for o in sorted(range(OWNERS), key=lambda o, c=c: rank_of(o, c))]
    for c, h in QUARTERS
]


def moves(shift, core, half):
    return [
        (device_of(o, c, h), device_of(o + shift, c ^ core, h ^ half))
        for o in range(OWNERS)
        for c, h in QUARTERS
    ]


X_SWAP = moves(0, 0, 1)
C_SWAP = moves(0, 1, 0)
DOWN = moves(-1, 0, 0)


def iota(shape, dim):
    return lax.broadcasted_iota(jnp.int32, shape, dim)


def nt(a, b):
    return lax.dot_general(a, b, (((1,), (1,)), ((), ())), preferred_element_type=F32)


def ones_where(mask):
    return jnp.where(mask, 1.0, 0.0).astype(BF16)


def pack_kernel(x_ref, cl_ref, ord_ref, map_ref, nbr_ref, out_ref, place_ref):
    clusters = cl_ref[...]
    orders = ord_ref[...]
    count = map_ref.shape[1]
    onehot = ones_where(iota((count, LOAD), 0) == clusters)
    first, second = nbr_ref[0:1, :], nbr_ref[1:2, :]
    row = iota((16, count), 0)
    owners = map_ref[...]
    core = lax.axis_index("shard") & 1
    table = jnp.where(row == 0, rank_of(owners, core), 0)
    table = jnp.where(row == 1, rank_of((owners + OWNERS - 1) & (OWNERS - 1), core), table)
    for at, value in enumerate((first >> 8, first & 255, second >> 8, second & 255)):
        table = jnp.where(row == 4 + at, value, table)
    looked = jnp.dot(table.astype(F32).astype(BF16), onehot, preferred_element_type=F32)
    owner = looked[0:1, :]
    across = jnp.broadcast_to(owner, (LOAD, LOAD))
    below = across.T
    before = iota((LOAD, LOAD), 0) < iota((LOAD, LOAD), 1)
    rank = jnp.sum(jnp.where((across == below) & before, 1.0, 0.0), axis=0, keepdims=True)
    row = iota((16, LOAD), 0)
    meta = jnp.where(row == 8, 1.0, jnp.where((row >= 4) & (row < 8), looked, 0.0))
    for at, value in enumerate((orders >> 8, orders & 255, clusters >> 8, clusters & 255)):
        meta = jnp.where(row == at, value.astype(F32), meta)
    meta = jnp.concatenate([meta, jnp.zeros((LANES - 16, LOAD), F32)], axis=0).astype(BF16)

    scaled = x_ref[...].astype(F32)
    mean_square = jnp.mean(scaled * scaled, axis=-1, keepdims=True)
    factor = lax.rsqrt(mean_square + 1e-06) * D ** (-0.5)
    unit = (scaled * factor).astype(BF16)

    slot = iota((QUART, LOAD), 0)
    target = slot >> 1
    pick = (owner == target.astype(F32)) & (rank == (slot & 1).astype(F32))
    pick = ones_where(pick)
    out_ref[:, 0:D] = jnp.dot(pick, unit, preferred_element_type=F32).astype(BF16)
    out_ref[:, D:WIDE] = nt(pick, meta).astype(BF16)
    row = iota((8, LOAD), 0)
    place_ref[...] = jnp.where(row == 0, owner, jnp.where(row == 1, looked[1:2, :], rank))


def key_meta(key_ref):
    row, lane = iota((16, LANES), 0), iota((16, LANES), 1)
    take = jnp.where(lane == 2 * row, 256.0, jnp.where(lane == 2 * row + 1, 1.0, 0.0))
    take = jnp.where(row < 4, take, jnp.where((row == 4) & (lane == 8), 1.0, 0.0))
    got = nt(take.astype(BF16), key_ref[:, D:WIDE])
    order = jnp.where(got[4:5, :] > 0.0, got[0:1, :], 1e9)
    return order, got[1:2, :], got[2:3, :], got[3:4, :]


def masked(scores, query, key):
    order, cluster, first, second = query
    related = (key[1] == cluster) | (key[1] == first) | (key[1] == second)
    return jnp.where(related & (key[0] < order), scores, -1.0)


def into_lanes(ref, first, base):
    lane = iota((OWNERS, LANES), 1)
    even, odd = (ref[pl.ds(k, OWNERS, stride=2), :] for k in range(2))
    return jnp.where(lane == first, even, jnp.where(lane == first + 1, odd, base))


def score_part(query, own_ref, own_key, high_ref, high_key, turn_ref):
    digits = query[:, D:WIDE].astype(F32)
    order, cluster, first, second = (
        digits[:, 2 * j : 2 * j + 1] * 256.0 + digits[:, 2 * j + 1 : 2 * j + 2] for j in range(4)
    )
    order = jnp.where(digits[:, 8:9] > 0.0, order, 1e9)
    meta = (order, cluster, first, second)
    rows = query[:, 0:D]
    best = masked(nt(rows, own_ref[:, 0:D]), meta, own_key)
    scores = nt(rows, high_ref[:, 0:D])
    best = jnp.maximum(best, masked(scores, meta, high_key))
    best = jnp.max(best, axis=1, keepdims=True)
    upper = jnp.max(masked(scores, high_key, meta), axis=0, keepdims=True)
    turn_ref[...] = jnp.broadcast_to(best, (QUART, LANES))
    return upper


def early_kernel(own_ref, far_ref, high_ref, out_ref, upper_ref, turn_ref):
    own_key, high_key = key_meta(own_ref), key_meta(high_ref)
    upper, found = None, -1.0
    for flip, query in enumerate((own_ref, far_ref)):
        over = score_part(query, own_ref, own_key, high_ref, high_key, turn_ref)
        found = into_lanes(turn_ref, 2 * flip, found)
        upper = over if upper is None else jnp.maximum(upper, over)
    out_ref[...] = found
    upper_ref[...] = jnp.broadcast_to(upper, (8, QUART))


def late_kernel(
    own_ref, core_ref, both_ref, high_ref, early_ref, over_ref, out_ref, upper_ref, turn_ref
):
    own_key, high_key = key_meta(own_ref), key_meta(high_ref)
    upper, found = over_ref[0:1, :], early_ref[...]
    for flip, query in ((2, core_ref), (3, both_ref)):
        over = score_part(query, own_ref, own_key, high_ref, high_key, turn_ref)
        found = into_lanes(turn_ref, 2 * flip, found)
        upper = jnp.maximum(upper, over)
    turn_ref[...] = jnp.broadcast_to(upper, (LANES, QUART)).T
    rows = into_lanes(turn_ref, 8, found).T
    upper_ref[...] = rows[8:16, :]
    device = lax.axis_index("shard") * X + lax.axis_index("rep")
    mine = ((device >> 2) & 1) * 2 + (((device >> 1) ^ device) & 1)
    for q in range(4):
        part = rows[0:2, :]
        for flip in range(1, 4):
            part = jnp.where((mine ^ q) == flip, rows[2 * flip : 2 * flip + 2, :], part)
        out_ref[pl.ds(8 * q, 8), :] = jnp.concatenate([part] * 4, axis=0)


def merge_kernel(got_ref, upper_ref, out_ref):
    best = got_ref[0:8, :]
    for q in range(1, 4):
        best = jnp.maximum(best, got_ref[pl.ds(8 * q, 8), :])
    rows = jnp.concatenate([best[0:2, :], upper_ref[0:2, :], best[0:4, :]], axis=0)
    out_ref[...] = jnp.concatenate([rows] * (OWNERS // 8), axis=0).T


def pick_kernel(got_ref, place_ref, out_ref):
    owner, lower, rank = place_ref[0:1, :], place_ref[1:2, :], place_ref[2:3, :]
    here = iota((OWNERS, LOAD), 0).astype(F32)
    best = got_ref[...]
    found = jnp.full((OWNERS, LOAD), -1.0, F32)
    for target, lane in ((owner, 0), (lower, 2)):
        values = jnp.where(rank == 0.0, best[:, lane : lane + 1], best[:, lane + 1 : lane + 2])
        found = jnp.maximum(found, jnp.where(target == here, values, -1.0))
    out_ref[...] = jnp.max(found, axis=0, keepdims=True)


def call(kernel, outs, scratch=(), flops=0, size=1 << 20):
    return pl.pallas_call(
        kernel,
        out_shape=outs,
        scratch_shapes=list(scratch),
        compiler_params=pltpu.CompilerParams(vmem_limit_bytes=24 << 20),
        cost_estimate=pl.CostEstimate(flops=flops, bytes_accessed=size, transcendentals=0),
    )


def shape(dims, dtype):
    return jax.ShapeDtypeStruct(dims, dtype)


def body(embeds, clusters, orders, owner_map, neighbours):
    packed, place = call(
        pack_kernel, [shape((QUART, WIDE), BF16), shape((8, LOAD), F32)], (), 10**8
    )(
        embeds,
        clusters.reshape(1, LOAD),
        orders.reshape(1, LOAD),
        owner_map.reshape(1, -1),
        neighbours.T,
    )
    got = lax.all_to_all(
        packed.reshape(OWNERS, 2, WIDE), AXES, 0, 0, axis_index_groups=GROUPS, tiled=True
    )
    own = got.reshape(QUART, WIDE)
    far = lax.ppermute(own, AXES, X_SWAP)
    high = lax.ppermute(own, AXES, DOWN)
    core = lax.ppermute(own, AXES, C_SWAP)
    both = lax.ppermute(far, AXES, C_SWAP)
    turn = [pltpu.VMEM((QUART, LANES), F32)]
    early, over = call(
        early_kernel,
        [shape((OWNERS, LANES), F32), shape((8, QUART), F32)],
        turn,
        6 * 10**8,
    )(own, far, high)
    best, upper = call(
        late_kernel, [shape((32, LANES), F32), shape((8, LANES), F32)], turn, 6 * 10**8
    )(own, core, both, high, early, over)
    met = lax.all_to_all(
        best.reshape(4, 8, LANES), AXES, 0, 0, axis_index_groups=OWNED, tiled=True
    )
    best = call(merge_kernel, shape((OWNERS, LANES), F32))(met.reshape(32, LANES), upper)
    back = lax.all_to_all(
        best.reshape(OWNERS, 1, LANES), AXES, 0, 0, axis_index_groups=GROUPS, tiled=True
    )
    return call(pick_kernel, shape((1, LOAD), F32))(
        back.reshape(OWNERS, LANES), place
    ).reshape(LOAD)


def solution(mesh):
    placed = (P(AXES, None), P(AXES), P(AXES), P(), P())
    return jax.shard_map(body, mesh=mesh, in_specs=placed, out_specs=P(AXES), check_vma=False)
```

```python
import jax
import jax.numpy as jnp
from jax import lax
from jax.experimental import pallas as pl
from jax.experimental.pallas import tpu as pltpu
from jax.sharding import PartitionSpec as P

AXES = ("shard", "rep")
Y, Z, X = 8, 8, 4
OWNERS = 128
LOAD = 128
D = 1024
LANES = 128
WIDE = D + LANES
QUART = 2 * OWNERS
F32, BF16 = jnp.float32, jnp.bfloat16


def device_of(owner, core, half):
    step, bit = divmod(owner % OWNERS, 2)
    y, z = divmod(step, Z)
    if y % 2:
        z = Z - 1 - z
    pair = bit ^ (step & 1)
    return ((y * Z + z) * 2 + core) * X + 2 * pair + (half ^ pair)


QUARTERS = [(core, half) for core in range(2) for half in range(2)]
OWNED = [[device_of(o, c, h) for c, h in QUARTERS] for o in range(OWNERS)]


def rank_of(owner, core):
    step = owner >> 1
    y = step >> 3
    z = (step & 7) ^ (7 * (y & 1))
    major, minor = y + core * (z - y), z + core * (y - z)
    return (((major * Z + minor) << 1) | ((owner ^ step) & 1)) ^ (core * (OWNERS - 1))


GROUPS = [
    [device_of(o, c, h) for o in sorted(range(OWNERS), key=lambda o, c=c: rank_of(o, c))]
    for c, h in QUARTERS
]


def moves(shift, core, half):
    return [
        (device_of(o, c, h), device_of(o + shift, c ^ core, h ^ half))
        for o in range(OWNERS)
        for c, h in QUARTERS
    ]


X_SWAP = moves(0, 0, 1)
C_SWAP = moves(0, 1, 0)
DOWN = moves(-1, 0, 0)


def iota(shape, dim):
    return lax.broadcasted_iota(jnp.int32, shape, dim)


def nt(a, b):
    return lax.dot_general(a, b, (((1,), (1,)), ((), ())), preferred_element_type=F32)


def ones_where(mask):
    return jnp.where(mask, 1.0, 0.0).astype(BF16)


def pack_kernel(
    x_hbm, cl_hbm, ord_hbm, map_hbm, nbr_hbm, out_ref, place_ref,
    x_ref, cl_ref, ord_ref, map_ref, nbr_ref, sems,
):
    pairs = (
        (cl_hbm, cl_ref),
        (map_hbm, map_ref),
        (nbr_hbm, nbr_ref),
        (ord_hbm, ord_ref),
        (x_hbm, x_ref),
    )
    copies = [pltpu.make_async_copy(a, b, sems.at[j]) for j, (a, b) in enumerate(pairs)]
    for copy in copies[::-1]:
        copy.start()
    for copy in copies[:4]:
        copy.wait()
    clusters = cl_ref[...]
    orders = ord_ref[...]
    count = map_ref.shape[1]
    onehot = ones_where(iota((count, LOAD), 0) == clusters)
    first, second = nbr_ref[0:1, :], nbr_ref[1:2, :]
    row = iota((16, count), 0)
    owners = map_ref[...]
    core = lax.axis_index("shard") & 1
    table = jnp.where(row == 0, rank_of(owners, core), 0)
    table = jnp.where(row == 1, rank_of((owners + OWNERS - 1) & (OWNERS - 1), core), table)
    for at, value in enumerate((first >> 8, first & 255, second >> 8, second & 255)):
        table = jnp.where(row == 4 + at, value, table)
    looked = jnp.dot(table.astype(F32).astype(BF16), onehot, preferred_element_type=F32)
    owner = looked[0:1, :]
    across = jnp.broadcast_to(owner, (LOAD, LOAD))
    below = across.T
    before = iota((LOAD, LOAD), 0) < iota((LOAD, LOAD), 1)
    rank = jnp.sum(jnp.where((across == below) & before, 1.0, 0.0), axis=0, keepdims=True)
    row = iota((16, LOAD), 0)
    meta = jnp.where(row == 8, 1.0, jnp.where((row >= 4) & (row < 8), looked, 0.0))
    for at, value in enumerate((orders >> 8, orders & 255, clusters >> 8, clusters & 255)):
        meta = jnp.where(row == at, value.astype(F32), meta)
    meta = jnp.concatenate([meta, jnp.zeros((LANES - 16, LOAD), F32)], axis=0).astype(BF16)

    copies[4].wait()
    scaled = x_ref[...].astype(F32)
    mean_square = jnp.mean(scaled * scaled, axis=-1, keepdims=True)
    factor = lax.rsqrt(mean_square + 1e-06) * D ** (-0.5)
    unit = (scaled * factor).astype(BF16)

    slot = iota((QUART, LOAD), 0)
    target = slot >> 1
    pick = (owner == target.astype(F32)) & (rank == (slot & 1).astype(F32))
    pick = ones_where(pick)
    out_ref[:, 0:D] = jnp.dot(pick, unit, preferred_element_type=F32).astype(BF16)
    out_ref[:, D:WIDE] = nt(pick, meta).astype(BF16)
    row = iota((8, LOAD), 0)
    place_ref[...] = jnp.where(row == 0, owner, jnp.where(row == 1, looked[1:2, :], rank))


def key_meta(key_ref):
    row, lane = iota((16, LANES), 0), iota((16, LANES), 1)
    take = jnp.where(lane == 2 * row, 256.0, jnp.where(lane == 2 * row + 1, 1.0, 0.0))
    take = jnp.where(row < 4, take, jnp.where((row == 4) & (lane == 8), 1.0, 0.0))
    got = nt(take.astype(BF16), key_ref[:, D:WIDE])
    order = jnp.where(got[4:5, :] > 0.0, got[0:1, :], 1e9)
    return order, got[1:2, :], got[2:3, :], got[3:4, :]


def masked(scores, query, key):
    order, cluster, first, second = query
    related = (key[1] == cluster) | (key[1] == first) | (key[1] == second)
    return jnp.where(related & (key[0] < order), scores, -1.0)


def into_lanes(ref, first, base):
    lane = iota((OWNERS, LANES), 1)
    even, odd = (ref[pl.ds(k, OWNERS, stride=2), :] for k in range(2))
    return jnp.where(lane == first, even, jnp.where(lane == first + 1, odd, base))


def score_part(query, own_ref, own_key, high_ref, high_key, turn_ref):
    digits = query[:, D:WIDE].astype(F32)
    order, cluster, first, second = (
        digits[:, 2 * j : 2 * j + 1] * 256.0 + digits[:, 2 * j + 1 : 2 * j + 2] for j in range(4)
    )
    order = jnp.where(digits[:, 8:9] > 0.0, order, 1e9)
    meta = (order, cluster, first, second)
    rows = query[:, 0:D]
    best = masked(nt(rows, own_ref[:, 0:D]), meta, own_key)
    scores = nt(rows, high_ref[:, 0:D])
    best = jnp.maximum(best, masked(scores, meta, high_key))
    best = jnp.max(best, axis=1, keepdims=True)
    upper = jnp.max(masked(scores, high_key, meta), axis=0, keepdims=True)
    turn_ref[...] = jnp.broadcast_to(best, (QUART, LANES))
    return upper


def early_kernel(own_ref, far_ref, high_ref, out_ref, upper_ref, turn_ref):
    own_key, high_key = key_meta(own_ref), key_meta(high_ref)
    upper, found = None, -1.0
    for flip, query in enumerate((own_ref, far_ref)):
        over = score_part(query, own_ref, own_key, high_ref, high_key, turn_ref)
        found = into_lanes(turn_ref, 2 * flip, found)
        upper = over if upper is None else jnp.maximum(upper, over)
    out_ref[...] = found
    upper_ref[...] = jnp.broadcast_to(upper, (8, QUART))


def late_kernel(
    own_ref, core_ref, both_ref, high_ref, early_ref, over_ref, out_ref, upper_ref, turn_ref
):
    own_key, high_key = key_meta(own_ref), key_meta(high_ref)
    upper, found = over_ref[0:1, :], early_ref[...]
    for flip, query in ((2, core_ref), (3, both_ref)):
        over = score_part(query, own_ref, own_key, high_ref, high_key, turn_ref)
        found = into_lanes(turn_ref, 2 * flip, found)
        upper = jnp.maximum(upper, over)
    turn_ref[...] = jnp.broadcast_to(upper, (LANES, QUART)).T
    rows = into_lanes(turn_ref, 8, found).T
    upper_ref[...] = rows[8:16, :]
    device = lax.axis_index("shard") * X + lax.axis_index("rep")
    mine = ((device >> 2) & 1) * 2 + (((device >> 1) ^ device) & 1)
    for q in range(4):
        part = rows[0:2, :]
        for flip in range(1, 4):
            part = jnp.where((mine ^ q) == flip, rows[2 * flip : 2 * flip + 2, :], part)
        out_ref[pl.ds(8 * q, 8), :] = jnp.concatenate([part] * 4, axis=0)


def merge_kernel(got_ref, upper_ref, out_ref):
    best = got_ref[0:8, :]
    for q in range(1, 4):
        best = jnp.maximum(best, got_ref[pl.ds(8 * q, 8), :])
    rows = jnp.concatenate([best[0:2, :], upper_ref[0:2, :], best[0:4, :]], axis=0)
    out_ref[...] = jnp.concatenate([rows] * (OWNERS // 8), axis=0).T


def pick_kernel(got_ref, place_ref, out_ref):
    owner, lower, rank = place_ref[0:1, :], place_ref[1:2, :], place_ref[2:3, :]
    here = iota((OWNERS, LOAD), 0).astype(F32)
    best = got_ref[...]
    found = jnp.full((OWNERS, LOAD), -1.0, F32)
    for target, lane in ((owner, 0), (lower, 2)):
        values = jnp.where(rank == 0.0, best[:, lane : lane + 1], best[:, lane + 1 : lane + 2])
        found = jnp.maximum(found, jnp.where(target == here, values, -1.0))
    out_ref[...] = jnp.max(found, axis=0, keepdims=True)


def call(kernel, outs, scratch=(), flops=0, vmem=24, **more):
    return pl.pallas_call(
        kernel,
        **more,
        out_shape=outs,
        scratch_shapes=list(scratch),
        compiler_params=pltpu.CompilerParams(vmem_limit_bytes=vmem << 20),
        cost_estimate=pl.CostEstimate(flops=flops, bytes_accessed=1 << 20, transcendentals=0),
    )


def shape(dims, dtype):
    return jax.ShapeDtypeStruct(dims, dtype)


def body(embeds, clusters, orders, owner_map, neighbours):
    held = (
        embeds,
        clusters.reshape(1, LOAD),
        orders.reshape(1, LOAD),
        owner_map.reshape(1, -1),
        neighbours.T,
    )
    packed, place = call(
        pack_kernel,
        [shape((QUART, WIDE), BF16), shape((8, LOAD), F32)],
        [pltpu.VMEM(a.shape, a.dtype) for a in held] + [pltpu.SemaphoreType.DMA((5,))],
        10**8,
        vmem=60,
        in_specs=[pl.BlockSpec(memory_space=pltpu.HBM)] * 5,
    )(*held)
    got = lax.all_to_all(
        packed.reshape(OWNERS, 2, WIDE), AXES, 0, 0, axis_index_groups=GROUPS, tiled=True
    )
    own = got.reshape(QUART, WIDE)
    far = lax.ppermute(own, AXES, X_SWAP)
    high = lax.ppermute(own, AXES, DOWN)
    core = lax.ppermute(own, AXES, C_SWAP)
    both = lax.ppermute(far, AXES, C_SWAP)
    turn = [pltpu.VMEM((QUART, LANES), F32)]
    early, over = call(
        early_kernel,
        [shape((OWNERS, LANES), F32), shape((8, QUART), F32)],
        turn,
        6 * 10**8,
    )(own, far, high)
    best, upper = call(
        late_kernel, [shape((32, LANES), F32), shape((8, LANES), F32)], turn, 6 * 10**8
    )(own, core, both, high, early, over)
    met = lax.all_to_all(
        best.reshape(4, 8, LANES), AXES, 0, 0, axis_index_groups=OWNED, tiled=True
    )
    best = call(merge_kernel, shape((OWNERS, LANES), F32))(met.reshape(32, LANES), upper)
    back = lax.all_to_all(
        best.reshape(OWNERS, 1, LANES), AXES, 0, 0, axis_index_groups=GROUPS, tiled=True
    )
    return call(pick_kernel, shape((1, LOAD), F32))(
        back.reshape(OWNERS, LANES), place
    ).reshape(LOAD)


def solution(mesh):
    placed = (P(AXES, None), P(AXES), P(AXES), P(), P())
    return jax.shard_map(body, mesh=mesh, in_specs=placed, out_specs=P(AXES), check_vma=False)
```
